256 devices in a mesh: band: 64 (over y, z, core), chan: 4 (over x).
Axes of the slice: x: 4, y: 4, z: 8, core: 2. Of those that a mesh axis runs over, the one named last changes fastest.
Arguments:
- grid_in: bfloat16 [474, 65536], P(None, 'band'), may hold values from -6 to 6
- w_grid: bfloat16 [474, 512], P(None, 'chan'), may hold values from -0.25 to 0.25
- mesh_in: bfloat16 [512, 32768], P('chan', 'band'), may hold values from -6 to 6
- g2m_attr: bfloat16 [4, 524288], P(None, 'band'), may hold values from -6 to 6
- g2m_send: int32 [320, 512], P('band'), may hold values from 0 to 1023
- g2m_src: int32 [524288], P('band'), may hold values from 0 to 2559, as said below
- g2m_dst: int32 [524288], P('band'), may hold values from -1 to 511, as said below
- w_gs: bfloat16 [512, 512], P(None, 'chan'), may hold values from -0.25 to 0.25
- w_gr: bfloat16 [512, 512], P(None, 'chan'), may hold values from -0.25 to 0.25
- w_ge: bfloat16 [4, 512], P(None, 'chan'), may hold values from -3 to 3
- w_nm: bfloat16 [512, 512], P('chan'), may hold values from -0.25 to 0.25
- w_na: bfloat16 [512, 512], P('chan'), may hold values from -0.09375 to 0.09375
- w_no: bfloat16 [512, 512], P('chan'), may hold values from -1.767767 to 1.767767
- gain_enc: float32 [512], P('chan'), may hold values from 0.1 to 1.9
- mesh_attr: bfloat16 [4, 262144], P(None, 'band'), may hold values from -6 to 6
- mesh_send: int32 [320, 256], P('band'), may hold values from 0 to 511
- mesh_src: int32 [262144], P('band'), may hold values from 0 to 1279, as said below
- mesh_dst: int32 [262144], P('band'), may hold values from 0 to 511, as said below
- w_ms: bfloat16 [512, 512], P(None, 'chan'), may hold values from -0.25 to 0.25
- w_mr: bfloat16 [512, 512], P(None, 'chan'), may hold values from -0.25 to 0.25
- w_me: bfloat16 [4, 512], P(None, 'chan'), may hold values from -3 to 3
- w_pm: bfloat16 [512, 512], P('chan'), may hold values from -0.25 to 0.25
- w_pa: bfloat16 [512, 512], P('chan'), may hold values from -0.125 to 0.125
- w_po: bfloat16 [512, 512], P('chan'), may hold values from -1.767767 to 1.767767
- gain_proc: float32 [512], P('chan'), may hold values from 0.1 to 1.9
- cotangent: bfloat16 [512, 32768], P('chan', 'band'), may hold values from -6 to 6
Outputs:
- mesh_out: bfloat16 [512, 32768], P('chan', 'band')
- mesh_grad: float32 [512, 32768], P('chan', 'band')
- w_grid_grad: float32 [474, 512], P(None, 'chan')
The draws below stay inside these ranges and needn't reach their ends.
Inputs may be any that keep to these rules, and one draw needn't show every extreme that they name: `g2m_dst`: each device's 8192 slots hold its live edges first, sorted by receiver, then -1 in the rest; receivers 0 and 511 occur on every device; the first and last band devices are full, and every device has at least 819 live edges. `g2m_src`: column b names slot j = b // 512 of the device's table; live edges name only slots j whose source device d + 2 - j exists. `mesh_dst`: each device's 4096 edges are sorted by receiver; receivers 0 and 511 occur on every device. `mesh_src`: column b names slot j = b // 256; edges name only slots j whose source device d + 2 - j exists.
All inputs are finite; a program needn't handle non-finite values.
Results may differ from the reference program's by a relative error of at most 0.035.
Values may be sent and summed in bfloat16 or wider, within the bound.
A program may use at most 128 MiB of HBM per device.

```python
import jax
import jax.numpy as jnp
from jax import lax

L = 512
FIN = 474
EA = 4
OFFS = 5
GRID_DEV = 1024
MESH_DEV = 512
G2M_DEV = 8192
MEDGE_DEV = 4096
CAP = 512
MCAP = 256
GRID = 65536
MESH = 32768
EDGES = 524288
MEDGES = 262144
N_BAND = 64


def live_slots(devices, slot_count):
    device = jnp.arange(devices, dtype=jnp.int32)
    extent = max(devices - 1, 1)
    offset = 2 * device - (devices - 1)
    return slot_count * (extent * extent + 9 * offset * offset) // (10 * extent * extent)


def sorted_targets(key, devices, slot_count, receivers, live_rows):
    sampled = jax.random.randint(key, (devices, slot_count), 0, receivers, dtype=jnp.int32)
    sampled = sampled.at[:, 0].set(0).at[:, 1].set(receivers - 1)
    present = jnp.arange(slot_count, dtype=jnp.int32)[None, :] < live_rows[:, None]
    ordered = jnp.sort(jnp.where(present, sampled, receivers), axis=1)
    return jnp.where(ordered < receivers, ordered, -1).reshape(devices * slot_count)


def table_slots(key, devices, slot_count, capacity):
    radius = (OFFS - 1) // 2
    slot_key, column_key = jax.random.split(key)
    chosen = jax.random.randint(slot_key, (devices, slot_count), 0, OFFS, dtype=jnp.int32)
    column = jax.random.randint(column_key, (devices, slot_count), 0, capacity, dtype=jnp.int32)
    source = jnp.arange(devices, dtype=jnp.int32)[:, None] + radius - chosen
    chosen = jnp.where((source < 0) | (source >= devices), 2 * radius - chosen, chosen)
    return (chosen * capacity + column).reshape(devices * slot_count)


def column_scaled(base, top_ratio):
    width = base.shape[1]
    position = jnp.arange(width, dtype=jnp.float32) / float(max(width - 1, 1))
    factor = jnp.exp(jnp.log(top_ratio) * position)
    return base * factor[None, :] * float(base.shape[0]) ** (-0.5)


def draw_output_weight(key):
    base = jax.random.truncated_normal(key, -4.0, 4.0, (L, L), jnp.float32)
    return column_scaled(base, 6.0).astype(jnp.bfloat16)


def draw_w_no(key, part):
    key = jax.random.fold_in(key, 25)
    return draw_output_weight(key)


def draw_w_po(key, part):
    key = jax.random.fold_in(key, 26)
    return draw_output_weight(key)


def draw_g2m_src(key, part):
    key = jax.random.fold_in(key, 21)
    return table_slots(key, EDGES // G2M_DEV, G2M_DEV, CAP)


def draw_g2m_dst(key, part):
    key = jax.random.fold_in(key, 22)
    devices = EDGES // G2M_DEV
    return sorted_targets(key, devices, G2M_DEV, MESH_DEV, live_slots(devices, G2M_DEV))


def draw_mesh_src(key, part):
    key = jax.random.fold_in(key, 23)
    return table_slots(key, MEDGES // MEDGE_DEV, MEDGE_DEV, MCAP)


def draw_mesh_dst(key, part):
    key = jax.random.fold_in(key, 24)
    devices = MEDGES // MEDGE_DEV
    return sorted_targets(key, devices, MEDGE_DEV, MESH_DEV, jnp.full((devices,), MEDGE_DEV, jnp.int32))


def with_ends(drawn, key, low, largest):
    shape = drawn.shape
    spot = [jax.random.randint(jax.random.fold_in(key, axis), (), 0, shape[axis]) for axis in range(len(shape))]
    drawn = drawn.at[tuple(spot)].set(low)
    longest = shape.index(max(shape))
    spot[longest] = (spot[longest] + 1) % shape[longest]
    return drawn.at[tuple(spot)].set(largest)


def block_levels(stream_key, dims, cuts, least, largest):
    def one(axis_at, blocks):
        draws = jax.random.uniform(jax.random.fold_in(jax.random.fold_in(stream_key, 6), axis_at), (blocks,), jnp.float32, least / len(cuts), largest / len(cuts))
        return jnp.repeat(jnp.exp(draws), dims[axis_at] // blocks).reshape((-1,) + (1,) * (len(dims) - axis_at - 1))

    loudness = one(*cuts[0])
    for cut in cuts[1:]:
        loudness = loudness * one(*cut)
    return loudness


def normal_values(own_key, shape, deviation, bound, pieces=(), kind=jnp.bfloat16):
    level = block_levels(own_key, shape, pieces, -0.22, 0.18) if pieces else 1.0
    array = jax.random.normal(own_key, shape, jnp.float32) * deviation * level
    return jnp.minimum(jnp.maximum(array, -bound), bound).astype(kind)


def setup_inputs(seed: int = 0) -> dict:
    key_of = jax.random.split(jax.random.key(seed), 27)
    return {
        "grid_in": normal_values(key_of[0], (FIN, GRID), 1.0, 6.0, ((1, 64),)),
        "w_grid": normal_values(key_of[1], (FIN, L), FIN ** -0.5, 0.25, ((1, 4),)),
        "mesh_in": normal_values(key_of[2], (L, MESH), 1.0, 6.0, ((0, 4), (1, 64))),
        "g2m_attr": normal_values(key_of[3], (EA, EDGES), 1.0, 6.0, ((1, 64),)),
        "g2m_send": with_ends(jax.random.randint(key_of[4], (OFFS * N_BAND, CAP), 0, GRID_DEV), jax.random.fold_in(key_of[4], 1), 0, GRID_DEV - 1).astype(jnp.int32),
        "g2m_src": draw_g2m_src(jax.random.fold_in(key_of[26], 71), 0),
        "g2m_dst": draw_g2m_dst(jax.random.fold_in(key_of[26], 71), 0),
        "w_gs": normal_values(key_of[7], (L, L), L ** -0.5, 0.25, ((1, 4),)),
        "w_gr": normal_values(key_of[8], (L, L), L ** -0.5, 0.25, ((1, 4),)),
        "w_ge": normal_values(key_of[9], (EA, L), EA ** -0.5, 3.0, ((1, 4),)),
        "w_nm": normal_values(key_of[10], (L, L), L ** -0.5, 0.25, ((0, 4),)),
        "w_na": normal_values(key_of[11], (L, L), (8 * L) ** -0.5, 0.09375, ((0, 4),)),
        "w_no": draw_w_no(jax.random.fold_in(key_of[26], 71), 0),
        "gain_enc": jnp.clip(1.0 + 0.18 * jax.random.normal(key_of[13], (L,), jnp.float32), 0.1, 1.9),
        "mesh_attr": normal_values(key_of[14], (EA, MEDGES), 1.0, 6.0, ((1, 64),)),
        "mesh_send": with_ends(jax.random.randint(key_of[15], (OFFS * N_BAND, MCAP), 0, MESH_DEV), jax.random.fold_in(key_of[15], 1), 0, MESH_DEV - 1).astype(jnp.int32),
        "mesh_src": draw_mesh_src(jax.random.fold_in(key_of[26], 71), 0),
        "mesh_dst": draw_mesh_dst(jax.random.fold_in(key_of[26], 71), 0),
        "w_ms": normal_values(key_of[18], (L, L), L ** -0.5, 0.25, ((1, 4),)),
        "w_mr": normal_values(key_of[19], (L, L), L ** -0.5, 0.25, ((1, 4),)),
        "w_me": normal_values(key_of[20], (EA, L), EA ** -0.5, 3.0, ((1, 4),)),
        "w_pm": normal_values(key_of[21], (L, L), L ** -0.5, 0.25, ((0, 4),)),
        "w_pa": normal_values(key_of[22], (L, L), (4 * L) ** -0.5, 0.125, ((0, 4),)),
        "w_po": draw_w_po(jax.random.fold_in(key_of[26], 71), 0),
        "gain_proc": jnp.clip(1.0 + 0.18 * jax.random.normal(key_of[24], (L,), jnp.float32), 0.1, 1.9),
        "cotangent": normal_values(key_of[25], (L, MESH), 1.0, 6.0, ((0, 4), (1, 64))),
    }


eps = 1e-05

def silu_grad(values):
    sigmoid_v = jax.nn.sigmoid(values)
    return sigmoid_v * (1.0 + values * (1.0 - sigmoid_v))

def contract(weight, field_in):
    return lax.dot_general(weight, field_in, (((0,), (0,)), ((), ())), preferred_element_type=jnp.float32)

def expand(weight, grad_in):
    return jnp.dot(weight, grad_in, preferred_element_type=jnp.float32)

def rounded_sum(values, label_ids, segments):
    widened = lax.optimization_barrier(values).astype(jnp.float32)
    return jax.ops.segment_sum(widened.T, label_ids, num_segments=segments).T

def source_rows(send_lists, rows_dev):
    capacity = send_lists.shape[1]
    radius = (OFFS - 1) // 2
    table = send_lists.reshape(N_BAND, OFFS, capacity)
    device = jnp.arange(N_BAND, dtype=jnp.int32)[:, None, None]
    slot_id = jnp.arange(OFFS, dtype=jnp.int32)[None, :, None]
    column = jnp.arange(capacity, dtype=jnp.int32)[None, None, :]
    source = device + radius - slot_id
    valid = (source >= 0) & (source < N_BAND)
    clipped = jnp.clip(source, 0, N_BAND - 1)
    row_ids = clipped * rows_dev + table[clipped, slot_id, column]
    valid = jnp.broadcast_to(valid, (N_BAND, OFFS, capacity))
    return (row_ids.reshape(N_BAND, OFFS * capacity), valid.reshape(N_BAND, OFFS * capacity))

def split_edges(sources, targets, features):
    per_device = sources.shape[0] // N_BAND
    return (sources.reshape(N_BAND, per_device), targets.reshape(N_BAND, per_device), jnp.moveaxis(features.reshape(features.shape[0], N_BAND, per_device), 1, 0))

def edge_terms(senders, recv_terms, w_send, w_edge, ids_dev, ok_dev, src_dev, dst_dev, feat_dev, device, mesh_dev):
    picked = jnp.where(ok_dev[None, :], jnp.take(senders, ids_dev, axis=1), jnp.zeros((), senders.dtype))
    local = lax.dynamic_slice_in_dim(recv_terms, device * mesh_dev, mesh_dev, 1)
    present = dst_dev >= 0
    anchors = jnp.where(present, dst_dev, 0)
    pre_act = jnp.take(contract(w_send, picked), src_dev, axis=1) + jnp.take(local, anchors, axis=1) + contract(w_edge, feat_dev)
    return (pre_act, present, anchors)

def forward_edges(senders, receivers, send_lists, sources, targets, features, w_send, w_recv, w_edge, rows_dev):
    row_ids, row_ok = source_rows(send_lists, rows_dev)
    mesh_dev = receivers.shape[1] // N_BAND
    recv_terms = contract(w_recv, receivers)

    def one_device(bundle):
        device, ids_dev, ok_dev, src_dev, dst_dev, feat_dev = bundle
        pre_act, present, anchors = edge_terms(senders, recv_terms, w_send, w_edge, ids_dev, ok_dev, src_dev, dst_dev, feat_dev, device, mesh_dev)
        hidden = jnp.where(present[None, :], jax.nn.silu(pre_act).astype(jnp.bfloat16), jnp.zeros((), jnp.bfloat16))
        return rounded_sum(hidden, anchors, mesh_dev).astype(jnp.bfloat16)
    src_all, dst_all, feat_all = split_edges(sources, targets, features)
    device_sums = lax.map(one_device, (jnp.arange(N_BAND, dtype=jnp.int32), row_ids, row_ok, src_all, dst_all, feat_all))
    return jnp.moveaxis(device_sums, 0, 1).reshape(device_sums.shape[1], N_BAND * mesh_dev)

def backward_edges(senders, receivers, send_lists, sources, targets, features, w_send, w_recv, w_edge, rows_dev, d_gather):
    row_ids, row_ok = source_rows(send_lists, rows_dev)
    mesh_dev = receivers.shape[1] // N_BAND
    recv_terms = contract(w_recv, receivers)
    buffer_rows = row_ids.shape[1]

    def one_device(bundle):
        device, ids_dev, ok_dev, src_dev, dst_dev, feat_dev = bundle
        pre_act, present, anchors = edge_terms(senders, recv_terms, w_send, w_edge, ids_dev, ok_dev, src_dev, dst_dev, feat_dev, device, mesh_dev)
        local_grad = lax.dynamic_slice_in_dim(d_gather, device * mesh_dev, mesh_dev, 1)
        d_edges = jnp.where(present[None, :], jnp.take(local_grad, anchors, axis=1), 0.0)
        d_pre = (d_edges * silu_grad(pre_act)).astype(jnp.bfloat16)
        d_recv = expand(w_recv, rounded_sum(d_pre, anchors, mesh_dev).astype(jnp.bfloat16))
        d_rows = expand(w_send, rounded_sum(d_pre, src_dev, buffer_rows).astype(jnp.bfloat16))
        return (d_recv, jnp.where(ok_dev[None, :], d_rows, 0.0))
    src_all, dst_all, feat_all = split_edges(sources, targets, features)
    d_recv_all, d_rows_all = lax.map(one_device, (jnp.arange(N_BAND, dtype=jnp.int32), row_ids, row_ok, src_all, dst_all, feat_all))
    channels = d_rows_all.shape[1]
    d_recv = jnp.moveaxis(d_recv_all, 0, 1).reshape(channels, N_BAND * mesh_dev)
    flat_rows = jnp.moveaxis(d_rows_all, 0, 1).reshape(channels, N_BAND * buffer_rows)
    d_senders = jnp.zeros((channels, senders.shape[1]), jnp.float32).at[:, row_ids.reshape(-1)].add(flat_rows)
    return (d_recv, d_senders)

def layer_norm(outputs):
    average = lax.optimization_barrier(jnp.mean(outputs, axis=0, keepdims=True))
    variance = lax.optimization_barrier(jnp.mean(outputs * outputs, axis=0, keepdims=True)) - average * average
    inverse = lax.rsqrt(variance + eps)
    return ((outputs - average) * inverse, inverse)

def node_forward(latent, gathered, w_latent, w_gather, w_out, scale_gain):
    pre_hidden = contract(w_latent, latent) + contract(w_gather, gathered)
    hidden = jax.nn.silu(pre_hidden).astype(jnp.bfloat16)
    normed, inverse = layer_norm(contract(w_out, hidden))
    updated = (latent.astype(jnp.float32) + normed * scale_gain[:, None]).astype(jnp.bfloat16)
    return (updated, pre_hidden, normed, inverse)

def norm_back(grad_in, normed, inverse, scale_gain):
    scaled = grad_in * scale_gain[:, None]
    first_mean = lax.optimization_barrier(jnp.mean(scaled, axis=0, keepdims=True))
    second_mean = lax.optimization_barrier(jnp.mean(scaled * normed, axis=0, keepdims=True))
    return ((scaled - first_mean - normed * second_mean) * inverse).astype(jnp.bfloat16)

def reference(grid_in, w_grid, mesh_in, g2m_attr, g2m_send, g2m_src, g2m_dst, w_gs, w_gr, w_ge, w_nm, w_na, w_no, gain_enc, mesh_attr, mesh_send, mesh_src, mesh_dst, w_ms, w_mr, w_me, w_pm, w_pa, w_po, gain_proc, cotangent):
    grid_pre = contract(w_grid, grid_in)
    grid_lat = jax.nn.silu(grid_pre).astype(jnp.bfloat16)
    enc_gather = forward_edges(grid_lat, mesh_in, g2m_send, g2m_src, g2m_dst, g2m_attr, w_gs, w_gr, w_ge, GRID_DEV)
    mesh_mid, enc_hidden_pre, enc_normed, enc_inverse = node_forward(mesh_in, enc_gather, w_nm, w_na, w_no, gain_enc)
    proc_gather = forward_edges(mesh_mid, mesh_mid, mesh_send, mesh_src, mesh_dst, mesh_attr, w_ms, w_mr, w_me, MESH_DEV)
    mesh_out, proc_hidden_pre, proc_normed, proc_inverse = node_forward(mesh_mid, proc_gather, w_pm, w_pa, w_po, gain_proc)
    top_grad = cotangent.astype(jnp.float32)
    d_out = norm_back(top_grad, proc_normed, proc_inverse, gain_proc)
    d_pre = (expand(w_po, d_out) * silu_grad(proc_hidden_pre)).astype(jnp.bfloat16)
    d_recv, d_send = backward_edges(mesh_mid, mesh_mid, mesh_send, mesh_src, mesh_dst, mesh_attr, w_ms, w_mr, w_me, MESH_DEV, expand(w_pa, d_pre))
    d_mid = top_grad + expand(w_pm, d_pre) + d_recv + d_send
    d_out = norm_back(d_mid, enc_normed, enc_inverse, gain_enc)
    d_pre = (expand(w_no, d_out) * silu_grad(enc_hidden_pre)).astype(jnp.bfloat16)
    d_recv, d_grid = backward_edges(grid_lat, mesh_in, g2m_send, g2m_src, g2m_dst, g2m_attr, w_gs, w_gr, w_ge, GRID_DEV, expand(w_na, d_pre))
    mesh_grad = d_mid + expand(w_nm, d_pre) + d_recv
    d_grid_pre = (d_grid * silu_grad(grid_pre)).astype(jnp.bfloat16)
    w_grid_grad = lax.dot_general(grid_in, d_grid_pre, (((1,), (1,)), ((), ())), preferred_element_type=jnp.float32) * GRID ** (-0.5)
    return (mesh_out, mesh_grad, w_grid_grad)
```

```python
import functools

import jax
import jax.numpy as jnp
from jax import lax
from jax.experimental import pallas as pl
from jax.experimental.pallas import tpu as pltpu
from jax.sharding import PartitionSpec as P

eps = 1e-05
bf16 = jnp.bfloat16
f32 = jnp.float32
MESH = pl.DeviceIdType.MESH
SEMS = 192
INPUTS = (
    *("grid_in", "w_grid", "mesh_in", "g2m_attr", "g2m_send", "g2m_src", "g2m_dst"),
    *("w_gs", "w_gr", "w_ge", "w_nm", "w_na", "w_no", "gain_enc"),
    *("mesh_attr", "mesh_send", "mesh_src", "mesh_dst"),
    *("w_ms", "w_mr", "w_me", "w_pm", "w_pa", "w_po", "gain_proc", "cotangent"),
)


def dot(a, b):
    return jnp.dot(a, b, preferred_element_type=f32)


def dot_nt(a, b):
    return lax.dot_general(a, b, (((1,), (1,)), ((), ())), preferred_element_type=f32)


def flip(x):
    return jnp.transpose(x.astype(f32))


def sigmoid(v):
    return 0.5 + 0.5 * jnp.tanh(0.5 * v)


def one_hot(ids, count):
    rows = lax.broadcasted_iota(jnp.int16, (count, ids.shape[1]), 0)
    return jnp.where(rows == ids.astype(jnp.int16), jnp.ones((), bf16), jnp.zeros((), bf16))


def slots_of(ids, capacity, slots):
    slot = jnp.zeros_like(ids)
    for j in range(1, slots):
        slot = slot + (ids >= j * capacity).astype(jnp.int32)
    return slot, ids - slot * capacity


def halves_of(ids, half):
    upper = ids >= half
    return upper, jnp.where(upper, ids - half, ids)


def two_rows(x):
    half = x.shape[1] // 2
    return jnp.concatenate([x[:, :half], x[:, half:]], axis=0)


def norm(out):
    width = out.shape[1]
    mean = jnp.sum(out, axis=1, keepdims=True) / width
    var = jnp.sum(out * out, axis=1, keepdims=True) / width - mean * mean
    inverse = lax.rsqrt(var + eps)
    return (out - mean) * inverse, inverse


def norm_back(grad, normed, inverse, gain):
    width = grad.shape[1]
    u = grad * gain
    a = jnp.sum(u, axis=1, keepdims=True) / width
    b = jnp.sum(u * normed, axis=1, keepdims=True) / width
    return ((u - a - normed * b) * inverse).astype(bf16)


def kernel(
    nband, nchan, inner, scale,
    grid_hbm, w_grid_hbm, mesh_in, g2m_attr_hbm, g2m_send_hbm, g2m_src_hbm, g2m_dst_hbm,
    w_gs_hbm, w_gr_hbm, w_ge_hbm, w_nm, w_na, w_no, gain_enc_hbm,
    mesh_attr_hbm, mesh_send_hbm, mesh_src_hbm, mesh_dst_hbm,
    w_ms, w_mr, w_me_hbm, w_pm, w_pa, w_po, gain_proc_hbm, cotangent,
    mesh_out, mesh_grad, w_grid_grad,
    grid_in, w_grid, g2m_attr, g2m_send, g2m_src, g2m_dst, w_gs, w_gr, w_ge, gain_enc,
    mesh_attr, mesh_send, mesh_src, mesh_dst, w_me, gain_proc,
    gpad, wg_pad, wg_t, we_pad, attr_g, attr_m,
    mesh_full, gains, cot_rows,
    f_nm, f_na, f_no, f_pm, f_pa, f_po, f_gs, f_gr, f_ms, f_mr,
    sgrid, s_grid, halo_out, table, edge_grad, edge_back,
    acc, nbuf, enc_g,
    s_out, r_out, s_in, r_in, mid_s, m_halo_out, m_table, m_edge_grad, m_edge_back, m_nbuf, proc_g,
    mo_out, mo_in, dg_out, dg_in, rows_acc, m_back_out, m_back_in, mr_out, mr_in, h_out, h_in,
    de_out, de_in, g_rows_acc, g_back_out, g_back_in, er_out, er_in, mg_out, mg_in,
    dgrid_out, dgrid_in, dpre_out, dpre_in,
    part, rs1, mine, rs2, last, total,
    ssem, rsem, lsem,
):
    d, c = lax.axis_index("band"), lax.axis_index("chan")
    width, cb = w_gs.shape
    fin, grid_dev = grid_in.shape
    mesh_dev = mesh_in.shape[1]
    nb = mesh_dev // nchan
    gb = grid_dev // nchan
    half = mesh_dev // 2
    offs, cap = g2m_send.shape
    radius = offs // 2
    ea = w_ge.shape[0]
    count = [0]
    local_count = [0]
    started = []

    def at(index, size):
        return pl.ds(pl.multiple_of(index * size, size), size)

    def fetch_local(src, dst):
        copy = pltpu.make_async_copy(src, dst, lsem.at[local_count[0]])
        local_count[0] += 1
        copy.start()
        return copy

    def remote(src, dst, target):
        i = count[0]
        count[0] += 1
        copy = pltpu.make_async_remote_copy(
            src_ref=src, dst_ref=dst, send_sem=ssem.at[i], recv_sem=rsem.at[i],
            device_id=target, device_id_type=MESH,
        )
        copy.start()
        started.append(copy)
        return copy

    def sent(copies):
        for copy in copies:
            copy.wait_send()
            started[:] = [other for other in started if other is not copy]

    def arrive(copies):
        for copy in copies:
            copy.wait_recv()

    own_w_grid = fetch_local(w_grid_hbm, w_grid)
    own_w_gs = fetch_local(w_gs_hbm, w_gs)
    own_grid = fetch_local(grid_hbm, grid_in)
    own_mesh = fetch_local(mesh_in, mesh_full.at[at(c, cb), :])
    own_rest = [
        fetch_local(src, dst)
        for src, dst in (
            (g2m_send_hbm, g2m_send), (w_gr_hbm, w_gr), (w_ge_hbm, w_ge), (g2m_attr_hbm, g2m_attr),
            (g2m_src_hbm, g2m_src), (g2m_dst_hbm, g2m_dst), (gain_enc_hbm, gain_enc), (gain_proc_hbm, gain_proc),
            (mesh_attr_hbm, mesh_attr), (mesh_send_hbm, mesh_send), (mesh_src_hbm, mesh_src),
            (mesh_dst_hbm, mesh_dst), (w_me_hbm, w_me), (cotangent.at[:, at(c, nb)], cot_rows.at[at(c, cb), :]),
        )
    ]

    chan_peers = [lax.rem(c + k, nchan) for k in range(1, nchan)]

    def band_at(offset):
        return lax.rem(d + offset + nband, nband)

    near = [band_at(o) for o in range(-radius, radius + 1) if o != 0]
    group, place = d // inner, lax.rem(d, inner)
    inner_peers = [group * inner + lax.rem(place + k, inner) for k in range(1, inner)]
    outer = nband // inner
    outer_peers = [lax.rem(group + k, outer) * inner + place for k in range(1, outer)]
    barrier = pltpu.get_barrier_semaphore()
    for p in chan_peers:
        pl.semaphore_signal(barrier, inc=1, device_id={"chan": p}, device_id_type=MESH)
    for b in near + inner_peers + outer_peers:
        pl.semaphore_signal(barrier, inc=1, device_id={"band": b}, device_id_type=MESH)

    def to_chan(src_of, dst):
        return [remote(src_of(p), dst, {"chan": p}) for p in chan_peers]

    def swap_rows(src, dst):
        size, lanes = dst.shape[0], src.shape[1]
        copies = to_chan(lambda p: src.at[at(p, size), :], dst.at[:, at(c, lanes)])
        dst[:, at(c, lanes)] = src[at(c, size), :]
        return copies

    def swap_lanes(src, dst):
        size, lanes = src.shape[0], dst.shape[1]
        copies = to_chan(lambda p: src.at[:, at(p, lanes)], dst.at[at(c, size), :])
        dst[at(c, size), :] = src[:, at(c, lanes)]
        return copies

    tail = fin // 16 * 16
    wg_pad[tail:, :] = jnp.zeros((wg_pad.shape[0] - tail, cb), bf16)
    own_w_grid.wait()
    wg_pad[0:fin, :] = w_grid[...]
    wg_t[at(c, cb), :] = flip(wg_pad[...]).astype(bf16)
    pl.semaphore_wait(barrier, len(chan_peers) + len(near) + len(inner_peers) + len(outer_peers))

    core = lax.rem(d, 2)
    sibling = d + 1 - 2 * core

    def wg_half(p):
        return wg_t.at[at(2 * p + core, cb // 2), :]

    wg_copies = to_chan(lambda p: wg_half(c), wg_half(c))

    gpad[tail:, :] = jnp.zeros((gpad.shape[0] - tail, grid_dev), bf16)
    own_grid.wait()
    gpad[0:fin, :] = grid_in[...]
    own_w_gs.wait()
    wgs_t = flip(w_gs[...]).astype(bf16)
    own_mesh.wait()
    for copy in own_rest:
        copy.wait()
    sent(wg_copies)
    mesh_copies = to_chan(lambda p: mesh_in, mesh_full.at[at(c, cb), :])
    gains[c] = jnp.zeros(gains.shape[1:], f32)
    gains[c, 0:1, :] = gain_enc[...]
    gains[c, 1:2, :] = gain_proc[...]
    we_pad[...] = jnp.zeros_like(we_pad)
    we_pad[0:ea, :] = w_ge[...].astype(f32)
    wge_t = jnp.transpose(we_pad[...]).astype(bf16)
    we_pad[0:ea, :] = w_me[...].astype(f32)
    wme_t = jnp.transpose(we_pad[...]).astype(bf16)
    attr_g[...] = jnp.zeros_like(attr_g)
    attr_g[0:ea, :] = g2m_attr[...]
    attr_m[...] = jnp.zeros_like(attr_m)
    attr_m[0:ea, :] = mesh_attr[...]
    wgr_t = flip(w_gr[...]).astype(bf16)
    shared = []
    for k in range(1, nchan):
        arrive([wg_copies[k - 1]])
        piece = wg_half(lax.rem(c - k + nchan, nchan))
        shared.append(remote(piece, piece, {"band": sibling}))
    arrive(shared)

    step = min(256, grid_dev)

    @pl.loop(0, grid_dev // step)
    def _(t):
        cols = at(t, step)
        pre = dot(wg_t[...], gpad[:, cols])
        sig = sigmoid(pre)
        sgrid[:, cols] = sig * (1.0 + pre * (1.0 - sig))
        s_grid[:, cols] = dot(wgs_t, (pre * sig).astype(bf16)).astype(bf16)

    order = [j for o in range(radius, 0, -1) for j in (radius - o, radius + o)]
    passes = [order[i : i + 2] for i in range(0, len(order), 2)]

    def pack(field, send, out, dest):
        rows = field.shape[1]
        copies = []
        for j in order + [radius]:
            picked = dot(field[...], one_hot(send[j : j + 1, :], rows)).astype(bf16)
            if j == radius:
                dest[j * cb : (j + 1) * cb, :] = picked
            else:
                out[j] = picked
                copies.append(remote(out.at[j], dest.at[j * cb : (j + 1) * cb, :], {"band": band_at(j - radius)}))
        return copies

    halo = pack(s_grid, g2m_send, halo_out, table)

    def half_of(shard, full):
        if shard.shape[0] == cb:
            lanes = at(core, width // 2)
            return shard.at[:, lanes], full.at[at(c, cb), lanes], full.at[:, lanes]
        rows = at(core, width // 2)
        return shard.at[rows, :], full.at[rows, at(c, cb)], full.at[rows, :]

    def fetch(pairs):
        pending = []
        for shard, full in pairs:
            src, dst, whole = half_of(shard, full)
            own = fetch_local(src, dst)
            pending.append((own, to_chan(lambda p: src, dst), whole))
        return pending

    def share(pending):
        copies = []
        for own, inbound, whole in pending:
            own.wait()
            arrive(inbound)
            copies.append(remote(whole, whole, {"band": sibling}))
        return copies

    arrive(mesh_copies)
    group_a = fetch([(w_nm, f_nm), (w_na, f_na), (w_no, f_no), (w_ms, f_ms), (w_mr, f_mr)])
    gain_copies = to_chan(lambda p: gains.at[c], gains.at[c])
    cot_copies = to_chan(lambda p: cotangent.at[:, at(p, nb)], cot_rows.at[at(c, cb), :])

    def upper_lower(upper, x):
        return jnp.concatenate([jnp.where(upper, 0.0, x), jnp.where(upper, x, 0.0)], axis=0).astype(bf16)

    def pick_half(upper, pair):
        return jnp.where(upper, pair[cb:], pair[:cb])

    def edges_near(table, recv, w_edge_t, attr, src, dst, grads, tile):
        @pl.loop(0, src.shape[1] // tile)
        def _(t):
            cols = at(t, tile)
            slot, low = slots_of(src[:, cols], table.shape[1], offs)
            upper, node = halves_of(dst[:, cols], half)
            own = dot(table[radius * cb : (radius + 1) * cb, :], one_hot(low, table.shape[1]))
            pre = jnp.where(slot == radius, own, 0.0) + dot(w_edge_t, attr[:, cols])
            grads[:, cols] = pre + pick_half(upper, dot(recv, one_hot(node, half)))

    def edges_far(table, src, dst, grads, tile):
        acc[...] = jnp.zeros_like(acc)

        @pl.loop(0, src.shape[1] // tile)
        def _(t):
            cols = at(t, tile)
            slot, low = slots_of(src[:, cols], table.shape[1], offs)
            upper, node = halves_of(dst[:, cols], half)
            by_src = one_hot(low, table.shape[1])
            below = dot(table[: radius * cb, :], by_src)
            above = dot(table[(radius + 1) * cb :, :], by_src)
            sender = jnp.zeros((cb, tile), f32)
            for j in range(radius):
                sender = jnp.where(slot == j, below[j * cb : (j + 1) * cb, :], sender)
                sender = jnp.where(slot == j + radius + 1, above[j * cb : (j + 1) * cb, :], sender)
            pre = grads[:, cols] + sender
            sig = sigmoid(pre)
            grads[:, cols] = sig * (1.0 + pre * (1.0 - sig))
            acc[...] += dot_nt(one_hot(node, half), upper_lower(upper, pre * sig))

    def nodes_of(out):
        out[:half, :] = acc[:, :cb].astype(bf16)
        out[half:, :] = acc[:, cb:].astype(bf16)

    def edges_backward(grad, src, dst, grads, back, rows_ref, out, inbound, tile):
        capacity, tiles = rows_ref.shape[1], src.shape[1] // tile
        acc[...] = jnp.zeros_like(acc)
        rows_ref[...] = jnp.zeros_like(rows_ref)
        copies = []

        def add_rows(slots, base, cols, d_pre):
            slot, low = slots_of(src[:, cols], capacity, offs)
            slot = slot.astype(jnp.int16)
            parts = [jnp.where(slot == j, d_pre, jnp.zeros((), bf16)) for j in slots]
            rows_ref[base : base + len(slots) * cb, :] += dot_nt(
                jnp.concatenate(parts, axis=0) if len(parts) > 1 else parts[0], one_hot(low, capacity)
            )

        for i, slots in enumerate(passes):
            base = 2 * i * cb

            @pl.loop(0, tiles)
            def _(t):
                cols = at(t, tile)
                if i == 0:
                    upper, node = halves_of(dst[:, cols], half)
                    d_pre = pick_half(upper, dot(grad, one_hot(node, half))) * grads[:, cols]
                    back[:, cols] = d_pre.astype(bf16)
                add_rows(slots, base, cols, back[:, cols])

            for n, j in enumerate(slots):
                out[j] = rows_ref[base + n * cb : base + (n + 1) * cb, :].astype(bf16)
                copies.append(remote(out.at[j], inbound.at[j], {"band": band_at(radius - j)}))

        base = 2 * len(passes) * cb

        @pl.loop(0, tiles)
        def _(t):
            cols = at(t, tile)
            d_pre = back[:, cols]
            upper, node = halves_of(dst[:, cols], half)
            acc[...] += dot_nt(one_hot(node, half), upper_lower(upper, d_pre.astype(f32)))
            add_rows([radius], base, cols, d_pre)

        inbound[radius] = rows_ref[base : base + cb, :].astype(bf16)
        return copies

    tile_g = min(4096, g2m_src.shape[1])
    tile_m = min(4096, mesh_src.shape[1])
    recv_g = two_rows(dot(wgr_t, mesh_full[...]).astype(bf16))
    edges_near(table, recv_g, wge_t, attr_g, g2m_src, g2m_dst, edge_grad, tile_g)
    arrive(halo)
    edges_far(table, g2m_src, g2m_dst, edge_grad, tile_g)
    nodes_of(nbuf)
    enc_copies = swap_rows(nbuf, enc_g)
    a_copies = share(group_a)

    x = flip(mesh_full[:, at(c, nb)])
    arrive(gain_copies)
    gain_e = jnp.concatenate([gains[k, 0:1, :] for k in range(nchan)], axis=1)
    gain_p = jnp.concatenate([gains[k, 1:2, :] for k in range(nchan)], axis=1)
    arrive(a_copies)
    arrive(enc_copies)

    def mlp(latent, gathered, w_l, w_g, w_o):
        pre = dot(latent, w_l[...]) + dot(gathered[...], w_g[...])
        sig = sigmoid(pre)
        out = dot((pre * sig).astype(bf16), w_o[...])
        normed, inverse = norm(out)
        return sig * (1.0 + pre * (1.0 - sig)), normed, inverse

    enc_sg, enc_normed, enc_inverse = mlp(x.astype(bf16), enc_g, f_nm, f_na, f_no)
    mid = (x + enc_normed * gain_e).astype(bf16)
    s_out[...] = dot(mid, f_ms[...]).astype(bf16)
    s_copies = swap_lanes(s_out, s_in)
    r_out[...] = dot(mid, f_mr[...]).astype(bf16)
    r_copies = swap_lanes(r_out, r_in)

    arrive(s_copies)
    mid_s[...] = flip(s_in[...]).astype(bf16)
    m_halo = pack(mid_s, mesh_send, m_halo_out, m_table)
    arrive(r_copies)
    group_b = fetch([(w_pm, f_pm), (w_pa, f_pa), (w_po, f_po)])
    recv_m = two_rows(flip(r_in[...]).astype(bf16))
    edges_near(m_table, recv_m, wme_t, attr_m, mesh_src, mesh_dst, m_edge_grad, tile_m)
    arrive(m_halo)
    edges_far(m_table, mesh_src, mesh_dst, m_edge_grad, tile_m)
    nodes_of(m_nbuf)
    proc_copies = swap_rows(m_nbuf, proc_g)
    b_copies = share(group_b)
    arrive(cot_copies)
    cot = flip(cot_rows[...])
    arrive(b_copies)
    arrive(proc_copies)

    proc_sg, proc_normed, proc_inverse = mlp(mid, proc_g, f_pm, f_pa, f_po)
    d_out = norm_back(cot, proc_normed, proc_inverse, gain_p)
    d_hid = (dot_nt(d_out, f_po[...]) * proc_sg).astype(bf16)
    dg_out[...] = dot_nt(d_hid, f_pa[...]).astype(bf16)
    dg_copies = swap_lanes(dg_out, dg_in)
    mo_out[...] = flip(mid.astype(f32) + proc_normed * gain_p).astype(bf16)
    d_mid = cot + dot_nt(d_hid, f_pm[...])
    arrive(dg_copies)
    group_c = fetch([(w_gr, f_gr), (w_gs, f_gs)])
    mo_copies = swap_rows(mo_out, mo_in)
    m_back = edges_backward(
        two_rows(flip(dg_in[...]).astype(bf16)), mesh_src, mesh_dst, m_edge_grad, m_edge_back,
        rows_acc, m_back_out, m_back_in, tile_m,
    )
    nodes_of(mr_out)
    mr_copies = swap_rows(mr_out, mr_in)

    def gather_back(copies, inbound, add):
        value = add(radius, inbound[radius])
        for j, copy in zip(order, copies):
            arrive([copy])
            value = value + add(j, inbound[j])
        return value

    h_out[...] = gather_back(
        m_back, m_back_in, lambda j, rows: dot_nt(one_hot(mesh_send[j : j + 1, :], mesh_dev), rows)
    ).astype(bf16)
    h_copies = swap_rows(h_out, h_in)
    c_copies = share(group_c)
    arrive(mr_copies)
    d_mid = d_mid + dot_nt(mr_in[...], f_mr[...])
    arrive(h_copies)
    d_mid = d_mid + dot_nt(h_in[...], f_ms[...])

    d_out = norm_back(d_mid, enc_normed, enc_inverse, gain_e)
    d_hid = (dot_nt(d_out, f_no[...]) * enc_sg).astype(bf16)
    de_out[...] = dot_nt(d_hid, f_na[...]).astype(bf16)
    de_copies = swap_lanes(de_out, de_in)
    d_mesh = d_mid + dot_nt(d_hid, f_nm[...])
    arrive(de_copies)

    g_back = edges_backward(
        two_rows(flip(de_in[...]).astype(bf16)), g2m_src, g2m_dst, edge_grad, edge_back,
        g_rows_acc, g_back_out, g_back_in, tile_g,
    )
    nodes_of(er_out)
    er_copies = swap_rows(er_out, er_in)
    arrive(c_copies)
    dgrid_out[...] = gather_back(
        g_back, g_back_in, lambda j, rows: dot_nt(rows, one_hot(g2m_send[j : j + 1, :], grid_dev))
    ).astype(bf16)
    dgrid_copies = swap_lanes(dgrid_out, dgrid_in)
    arrive(er_copies)
    mg_out[...] = jnp.transpose(d_mesh + dot_nt(er_in[...], f_gr[...]))
    arrive(dgrid_copies)
    dpre_out[...] = (dot(f_gs[...], dgrid_in[...]) * sgrid[:, at(c, gb)]).astype(bf16)
    dpre_copies = swap_rows(dpre_out, dpre_in)
    arrive(mo_copies)
    mesh_out[...] = mo_in[...]
    arrive(dpre_copies)

    part[...] = dot_nt(gpad[...], dpre_in[...]).astype(bf16)
    piece = part.shape[0] // inner
    first = []
    for k in range(1, inner):
        q = lax.rem(place + k, inner)
        first.append(remote(part.at[at(q, piece), :], rs1.at[place], {"band": inner_peers[k - 1]}))
    mg_copies = swap_rows(mg_out, mg_in)
    rs1[place] = part[at(place, piece), :]
    arrive(first)
    mine[...] = jnp.sum(rs1[...].astype(f32), axis=0)
    rs2[group] = mine[...]
    second = [remote(mine, rs2.at[group], {"band": b}) for b in outer_peers]
    arrive(mg_copies)
    mesh_grad[...] = mg_in[...]
    arrive(second)
    last[...] = (jnp.sum(rs2[...], axis=0) * scale).astype(bf16)
    total[at(place, piece), :] = last[...]
    third = [remote(last, total.at[at(place, piece), :], {"band": b}) for b in inner_peers]
    arrive(third)
    w_grid_grad[...] = total[0:fin, :].astype(f32)
    for copy in started:
        copy.wait_send()


def local(nband, nchan, inner, *args):
    names = INPUTS
    a = dict(zip(names, args))
    for name in ("g2m_src", "g2m_dst", "mesh_src", "mesh_dst", "gain_enc", "gain_proc"):
        a[name] = a[name].reshape(1, -1)
    fin, grid_dev = a["grid_in"].shape
    width, cb = a["w_gs"].shape
    mesh_dev = a["mesh_in"].shape[1]
    nb, gb = mesh_dev // nchan, grid_dev // nchan
    offs, cap = a["g2m_send"].shape
    mcap = a["mesh_send"].shape[1]
    edges, medges = a["g2m_src"].shape[1], a["mesh_src"].shape[1]
    fp = -(-fin // 128) * 128
    scale = float(grid_dev * nband) ** (-0.5)
    v = pltpu.VMEM
    full = v((width, width), bf16)
    nodes = v((mesh_dev, cb), bf16)
    block = v((nb, width), bf16)
    held = [
        *("grid_in", "w_grid", "g2m_attr", "g2m_send", "g2m_src", "g2m_dst", "w_gs", "w_gr", "w_ge", "gain_enc"),
        *("mesh_attr", "mesh_send", "mesh_src", "mesh_dst", "w_me", "gain_proc"),
    ]
    scratch = [
        *[v(a[name].shape, a[name].dtype) for name in held],
        v((fp, grid_dev), bf16), v((fp, cb), bf16), v((width, fp), bf16), v((16, cb), f32),
        v((16, edges), bf16), v((16, medges), bf16),
        v((width, mesh_dev), bf16), v((nchan, 8, cb), f32), v((width, nb), bf16),
        *[full] * 10,
        v((width, grid_dev), f32), v((cb, grid_dev), bf16), v((offs, cb, cap), bf16), v((offs * cb, cap), bf16),
        v((cb, edges), f32), v((cb, edges), bf16),
        v((mesh_dev // 2, 2 * cb), f32), nodes, block,
        block, block, nodes, nodes, v((cb, mesh_dev), bf16), v((offs, cb, mcap), bf16), v((offs * cb, mcap), bf16),
        v((cb, medges), f32), v((cb, medges), bf16), nodes, block,
        v((width, nb), bf16), v((cb, mesh_dev), bf16), block, nodes, v((offs * cb, mcap), f32),
        v((offs, cb, mcap), bf16), v((offs, cb, mcap), bf16), nodes, block, nodes, block,
        block, nodes, v((offs * cb, cap), f32), v((offs, cb, cap), bf16), v((offs, cb, cap), bf16), nodes, block,
        v((width, nb), f32), v((cb, mesh_dev), f32),
        v((cb, grid_dev), bf16), v((width, gb), bf16), v((width, gb), bf16), v((cb, grid_dev), bf16),
        v((fp, cb), bf16), v((inner, fp // inner, cb), bf16), v((fp // inner, cb), f32),
        v((nband // inner, fp // inner, cb), f32), v((fp // inner, cb), bf16), v((fp, cb), bf16),
        pltpu.SemaphoreType.DMA((SEMS,)), pltpu.SemaphoreType.DMA((SEMS,)), pltpu.SemaphoreType.DMA((32,)),
    ]
    spec = pl.BlockSpec(memory_space=pltpu.VMEM)
    return pl.pallas_call(
        functools.partial(kernel, nband, nchan, inner, scale),
        out_shape=(
            jax.ShapeDtypeStruct((cb, mesh_dev), bf16),
            jax.ShapeDtypeStruct((cb, mesh_dev), f32),
            jax.ShapeDtypeStruct((fin, cb), f32),
        ),
        in_specs=[pl.BlockSpec(memory_space=pl.ANY)] * len(names),
        out_specs=(spec,) * 3,
        scratch_shapes=scratch,
        compiler_params=pltpu.CompilerParams(
            collective_id=0, has_side_effects=True, vmem_limit_bytes=56 * 2**20
        ),
    )(*[a[name] for name in names])


def solution(mesh):
    nband, nchan = mesh.shape["band"], mesh.shape["chan"]
    inner = min(16, nband // 2)
    return jax.shard_map(
        functools.partial(local, nband, nchan, inner),
        mesh=mesh,
        in_specs=(
            P(None, "band"),
            P(None, "chan"),
            P("chan", "band"),
            P(None, "band"),
            P("band", None),
            P("band"),
            P("band"),
            P(None, "chan"),
            P(None, "chan"),
            P(None, "chan"),
            P("chan", None),
            P("chan", None),
            P("chan", None),
            P("chan"),
            P(None, "band"),
            P("band", None),
            P("band"),
            P("band"),
            P(None, "chan"),
            P(None, "chan"),
            P(None, "chan"),
            P("chan", None),
            P("chan", None),
            P("chan", None),
            P("chan"),
            P("chan", "band"),
        ),
        out_specs=(P("chan", "band"), P("chan", "band"), P(None, "chan")),
        check_vma=False,
    )
```

```python
import functools

import jax
import jax.numpy as jnp
from jax import lax
from jax.experimental import pallas as pl
from jax.experimental.pallas import tpu as pltpu
from jax.sharding import PartitionSpec as P

eps = 1e-05
bf16 = jnp.bfloat16
f32 = jnp.float32
MESH = pl.DeviceIdType.MESH
BATCHES, OWN = 40, 22
INPUTS = (
    *("grid_in", "w_grid", "mesh_in", "g2m_attr", "g2m_send", "g2m_src", "g2m_dst"),
    *("w_gs", "w_gr", "w_ge", "w_nm", "w_na", "w_no", "gain_enc"),
    *("mesh_attr", "mesh_send", "mesh_src", "mesh_dst"),
    *("w_ms", "w_mr", "w_me", "w_pm", "w_pa", "w_po", "gain_proc", "cotangent"),
)


def whole(f):
    return f[...].reshape(f.shape[0] * f.shape[1], f.shape[2])


def dot(a, b):
    return jnp.dot(a, b, preferred_element_type=f32)


def dot_nt(a, b):
    return lax.dot_general(a, b, (((1,), (1,)), ((), ())), preferred_element_type=f32)


def flip(x):
    return jnp.transpose(x.astype(f32))


def sigmoid(v):
    return 0.5 + 0.5 * jnp.tanh(0.5 * v)


def one_hot(ids, count):
    rows = lax.broadcasted_iota(jnp.int16, (count, ids.shape[1]), 0)
    return jnp.where(rows == ids.astype(jnp.int16), jnp.ones((), bf16), jnp.zeros((), bf16))


def slots_of(ids, capacity, slots):
    slot = jnp.zeros_like(ids)
    for j in range(1, slots):
        slot = slot + (ids >= j * capacity).astype(jnp.int32)
    return slot, ids - slot * capacity


def halves_of(ids, half):
    upper = ids >= half
    return upper, jnp.where(upper, ids - half, ids)


def two_rows(x):
    half = x.shape[1] // 2
    return jnp.concatenate([x[:, :half], x[:, half:]], axis=0)


def norm(out):
    width = out.shape[1]
    mean = jnp.sum(out, axis=1, keepdims=True) / width
    var = jnp.sum(out * out, axis=1, keepdims=True) / width - mean * mean
    inverse = lax.rsqrt(var + eps)
    return (out - mean) * inverse, inverse


def norm_back(grad, normed, inverse, gain):
    width = grad.shape[1]
    u = grad * gain
    a = jnp.sum(u, axis=1, keepdims=True) / width
    b = jnp.sum(u * normed, axis=1, keepdims=True) / width
    return ((u - a - normed * b) * inverse).astype(bf16)


def kernel(
    nband, nchan, inner, scale,
    grid_hbm, w_grid_hbm, mesh_in, g2m_attr_hbm, g2m_send_hbm, g2m_src_hbm, g2m_dst_hbm,
    w_gs_hbm, w_gr_hbm, w_ge_hbm, w_nm, w_na, w_no, gain_enc_hbm,
    mesh_attr_hbm, mesh_send_hbm, mesh_src_hbm, mesh_dst_hbm,
    w_ms, w_mr, w_me_hbm, w_pm, w_pa, w_po, gain_proc_hbm, cotangent,
    mesh_out, mesh_grad, w_grid_sum,
    grid_in, w_grid, g2m_attr, g2m_send, g2m_src, g2m_dst, w_gs, w_gr, w_ge, gain_enc,
    mesh_attr, mesh_send, mesh_src, mesh_dst, w_me, gain_proc,
    gpad, wg_pad, wg_t, we_pad, attr_g, attr_m,
    mesh_full, gains, cot_rows,
    f_all,
    sgrid, s_grid, halo_out, table, edge_grad, edge_back,
    acc, nbuf, enc_g,
    s_out, r_out, s_in, r_in, mid_s, m_halo_out, m_table, m_edge_grad, m_edge_back, m_nbuf, proc_g,
    mo_out, mo_in, dg_out, dg_in, rows_acc, m_back_out, m_back_in, mr_out, mr_in, h_out, h_in,
    de_out, de_in, g_rows_acc, g_back_out, g_back_in, er_out, er_in, mg_out, mg_in,
    dgrid_out, dgrid_in, dpre_out, dpre_in,
    part, pair_in, pair_sum, rs1, mine, rs2, total,
    ssem, rsem, lsem,
):
    d, c = lax.axis_index("band"), lax.axis_index("chan")
    core = lax.rem(d, 2)
    sibling = d + 1 - 2 * core
    width, cb = w_gs.shape
    fin, grid_dev = grid_in.shape
    mesh_dev = mesh_in.shape[1]
    nb = mesh_dev // nchan
    gb = grid_dev // nchan
    half = mesh_dev // 2
    offs, cap = g2m_send.shape
    radius = offs // 2
    ea = w_ge.shape[0]
    f_nm, f_na, f_no, f_ms, f_mr, f_pm, f_pa, f_po, f_gs, f_gr = (
        f_all.at[i] for i in range(10)
    )
    count = [0]
    local_count = [0]
    started = []

    def at(index, size):
        return pl.ds(pl.multiple_of(index * size, size), size)

    def fetch_local(src, dst):
        copy = pltpu.make_async_copy(src, dst, lsem.at[local_count[0]])
        local_count[0] += 1
        copy.start()
        return copy

    def wait_on(whole, i):
        return pltpu.make_async_remote_copy(
            src_ref=whole, dst_ref=whole, send_sem=ssem.at[i], recv_sem=rsem.at[i],
            device_id={"band": sibling}, device_id_type=MESH,
        )

    def send(sends, whole):
        i = count[0]
        count[0] += 1
        for src, dst, target in sends:
            pltpu.make_async_remote_copy(
                src_ref=src, dst_ref=dst, send_sem=ssem.at[i], recv_sem=rsem.at[i],
                device_id=target, device_id_type=MESH,
            ).start()
        batch = (whole, i)
        started.append(batch)
        return batch

    def sent(batch):
        wait_on(*batch).wait_send()
        started[:] = [other for other in started if other is not batch]

    def arrive(batch):
        wait_on(*batch).wait_recv()

    own_w_grid = fetch_local(w_grid_hbm, w_grid)
    own_w_gs = fetch_local(w_gs_hbm, w_gs)
    own_grid = fetch_local(grid_hbm, grid_in)
    own_mesh = fetch_local(mesh_in, mesh_full.at[at(c, cb), :])
    own_rest = [
        fetch_local(src, dst)
        for src, dst in (
            (g2m_send_hbm, g2m_send), (w_gr_hbm, w_gr), (w_ge_hbm, w_ge), (g2m_attr_hbm, g2m_attr),
            (g2m_src_hbm, g2m_src), (g2m_dst_hbm, g2m_dst), (gain_enc_hbm, gain_enc), (gain_proc_hbm, gain_proc),
            (mesh_attr_hbm, mesh_attr), (mesh_send_hbm, mesh_send), (mesh_src_hbm, mesh_src),
            (mesh_dst_hbm, mesh_dst), (w_me_hbm, w_me), (cotangent.at[:, at(c, nb)], cot_rows.at[at(c, cb), :]),
        )
    ]

    def far_first(size):
        return sorted(range(1, size), key=lambda k: -min(k, size - k))

    chan_peers = [lax.rem(c + k, nchan) for k in far_first(nchan)]

    def band_at(offset):
        return lax.rem(d + offset + nband, nband)

    near = [band_at(o) for o in range(-radius, radius + 1) if o != 0]
    group, place = d // inner, lax.rem(d, inner)
    row, rows = place // 2, inner // 2
    row_peers = [lax.rem(row + k, rows) for k in far_first(rows)]
    inner_peers = [group * inner + 2 * p + core for p in row_peers]
    outer = nband // inner
    outer_peers = [lax.rem(group + k, outer) * inner + place for k in far_first(outer)]
    met = near + inner_peers + outer_peers + [sibling]
    barrier = pltpu.get_barrier_semaphore()
    for p in chan_peers:
        pl.semaphore_signal(barrier, inc=1, device_id={"chan": p}, device_id_type=MESH)
    for b in met:
        pl.semaphore_signal(barrier, inc=1, device_id={"band": b}, device_id_type=MESH)

    others = nchan - 1

    def to_chan(src_of, dst, whole):
        return send([(src_of(p), dst, {"chan": p}) for p in chan_peers], whole)

    def swap_rows(src, dst):
        size, lanes = dst.shape[0], src.shape[1]
        batch = to_chan(lambda p: src.at[at(p, size), :], dst.at[:, at(c, lanes)], dst.at[:, : others * lanes])
        dst[:, at(c, lanes)] = src[at(c, size), :]
        return batch

    def swap_lanes(src, dst):
        size, lanes = src.shape[0], dst.shape[1]
        batch = to_chan(lambda p: src.at[:, at(p, lanes)], dst.at[at(c, size), :], dst.at[: others * size, :])
        dst[at(c, size), :] = src[:, at(c, lanes)]
        return batch

    tail = fin // 16 * 16
    wg_pad[tail:, :] = jnp.zeros((wg_pad.shape[0] - tail, cb), bf16)
    own_w_grid.wait()
    wg_pad[0:fin, :] = w_grid[...]
    wg_t[at(c, cb), :] = flip(wg_pad[...]).astype(bf16)
    pl.semaphore_wait(barrier, len(chan_peers) + len(met))

    def wg_half(p):
        return wg_t.at[at(2 * p + core, cb // 2), :]

    wg_copies = to_chan(lambda p: wg_half(c), wg_half(c), wg_t.at[: others * cb // 2, :])
    gains[c] = jnp.zeros(gains.shape[1:], f32)

    gpad[tail:, :] = jnp.zeros((gpad.shape[0] - tail, grid_dev), bf16)
    own_grid.wait()
    gpad[0:fin, :] = grid_in[...]
    own_w_gs.wait()
    wgs_t = flip(w_gs[...]).astype(bf16)
    own_mesh.wait()
    for copy in own_rest:
        copy.wait()
    sent(wg_copies)
    mesh_copies = to_chan(lambda p: mesh_in, mesh_full.at[at(c, cb), :], mesh_full.at[: others * cb, :])
    gains[c, 0:1, :] = gain_enc[...]
    gains[c, 1:2, :] = gain_proc[...]
    we_pad[...] = jnp.zeros_like(we_pad)
    we_pad[0:ea, :] = w_ge[...].astype(f32)
    wge_t = jnp.transpose(we_pad[...]).astype(bf16)
    we_pad[0:ea, :] = w_me[...].astype(f32)
    wme_t = jnp.transpose(we_pad[...]).astype(bf16)
    attr_g[...] = jnp.zeros_like(attr_g)
    attr_g[0:ea, :] = g2m_attr[...]
    attr_m[...] = jnp.zeros_like(attr_m)
    attr_m[0:ea, :] = mesh_attr[...]
    wgr_t = flip(w_gr[...]).astype(bf16)
    arrive(wg_copies)
    halves = [wg_half(p) for p in chan_peers]
    arrive(send([(half_block, half_block, {"band": sibling}) for half_block in halves], wg_t.at[: others * cb // 2, :]))

    step = min(256, grid_dev)

    @pl.loop(0, grid_dev // step)
    def _(t):
        cols = at(t, step)
        pre = dot(wg_t[...], gpad[:, cols])
        sig = sigmoid(pre)
        sgrid[:, cols] = sig * (1.0 + pre * (1.0 - sig))
        s_grid[:, cols] = dot(wgs_t, (pre * sig).astype(bf16)).astype(bf16)

    order = [j for o in range(radius, 0, -1) for j in (radius - o, radius + o)]
    passes = [order[i : i + 2] for i in range(0, len(order), 2)]

    def pack(field, lists, out, dest):
        def picked(j):
            return dot(field[...], one_hot(lists[j : j + 1, :], field.shape[1])).astype(bf16)

        def block(j):
            return dest.at[j * cb : (j + 1) * cb, :]

        def sends():
            for j in order:
                out[j] = picked(j)
                yield out.at[j], block(j), {"band": band_at(j - radius)}

        batch = send(sends(), dest.at[: (offs - 1) * cb, :])
        dest[radius * cb : (radius + 1) * cb, :] = picked(radius)
        return batch

    halo = pack(s_grid, g2m_send, halo_out, table)

    def part_of(shard, full, cuts):
        index = group if cuts > 1 else 0
        if shard.shape[0] == cb:
            rows, lanes = at(index, cb // cuts), at(core, width // 2)
            return shard.at[rows, lanes], full.at[c, rows, lanes], full.at[:, rows, lanes], full.at[:, :, lanes]
        blocks = at(core, nchan // 2)
        size = width // 2 // cuts
        if size >= cb:
            blocks, rows = at(core * cuts + index, size // cb), pl.ds(0, cb)
        else:
            first = (core * cuts + index) * size
            blocks, rows = pl.ds(first // cb, 1), pl.ds(pl.multiple_of(lax.rem(first, cb), size), size)
        source = shard.at[at(core * cuts + index, size), :]
        if size >= cb:
            source = [shard.at[at((core * cuts + index) * (size // cb) + n, cb), :] for n in range(size // cb)]
            target = [full.at[(core * cuts + index) * (size // cb) + n, :, at(c, cb)] for n in range(size // cb)]
        else:
            source, target = [source], [full.at[first // cb, rows, at(c, cb)]]
        return source, target, full.at[blocks, rows, :], full.at[at(core, nchan // 2), :, :]

    def listed(x):
        return x if isinstance(x, list) else [x]

    def fetch(pairs, cuts=1):
        sends, regions, halves, own = [], [], [], local_count[0]
        local_count[0] += 1
        for shard, full in pairs:
            src, dst, region, whole = part_of(shard, full, cuts)
            for one, other in zip(listed(src), listed(dst)):
                pltpu.make_async_copy(one, other, lsem.at[own]).start()
                sends += [(one, other, {"chan": p}) for p in chan_peers]
            regions.append(region)
            halves.append(whole)
        unit = cb // 2 // cuts
        size = len(pairs)
        return send(sends, f_all.at[:size, :others, :unit, :]), own, f_all.at[:size, 0, :unit, :], regions, halves

    def fetched(group_copies):
        inbound, own, own_whole, regions, halves = group_copies
        pltpu.make_async_copy(own_whole, own_whole, lsem.at[own]).wait()
        arrive(inbound)
        return regions, halves

    def relay(group_copies):
        regions, halves = fetched(group_copies)
        sends = [(r, r, {"band": b}) for r in regions for b in outer_peers]
        unit = nchan * cb // 2 // outer
        return send(sends, f_all.at[: len(regions), : outer - 1, :unit, :]), halves

    def share(halves):
        return send([(w, w, {"band": sibling}) for w in halves], f_all.at[: len(halves), : nchan // 2, :, :])

    def relayed(relay_copies):
        arrive(relay_copies[0])
        return share(relay_copies[1])

    sent(mesh_copies)
    gain_copies = to_chan(lambda p: gains.at[c], gains.at[c], gains.at[:others])
    group_m = fetch([(w_ms, f_ms), (w_mr, f_mr)], outer)
    group_a = fetch([(w_nm, f_nm), (w_na, f_na), (w_no, f_no)])
    group_b = fetch([(w_pm, f_pm), (w_pa, f_pa), (w_po, f_po)], outer)
    group_c = fetch([(w_gr, f_gr), (w_gs, f_gs)], outer)

    def upper_lower(upper, x):
        return jnp.concatenate([jnp.where(upper, 0.0, x), jnp.where(upper, x, 0.0)], axis=0).astype(bf16)

    def pick_half(upper, pair):
        return jnp.where(upper, pair[cb:], pair[:cb])

    def edges_near(table, recv, w_edge_t, attr, src, dst, grads, tile):
        @pl.loop(0, src.shape[1] // tile)
        def _(t):
            cols = at(t, tile)
            slot, low = slots_of(src[:, cols], table.shape[1], offs)
            upper, node = halves_of(dst[:, cols], half)
            own = dot(table[radius * cb : (radius + 1) * cb, :], one_hot(low, table.shape[1]))
            pre = jnp.where(slot == radius, own, 0.0) + dot(w_edge_t, attr[:, cols])
            grads[:, cols] = pre + pick_half(upper, dot(recv, one_hot(node, half)))

    def edges_far(table, src, dst, grads, tile):
        acc[...] = jnp.zeros_like(acc)

        @pl.loop(0, src.shape[1] // tile)
        def _(t):
            cols = at(t, tile)
            slot, low = slots_of(src[:, cols], table.shape[1], offs)
            upper, node = halves_of(dst[:, cols], half)
            by_src = one_hot(low, table.shape[1])
            below = dot(table[: radius * cb, :], by_src)
            above = dot(table[(radius + 1) * cb :, :], by_src)
            sender = jnp.zeros((cb, tile), f32)
            for j in range(radius):
                sender = jnp.where(slot == j, below[j * cb : (j + 1) * cb, :], sender)
                sender = jnp.where(slot == j + radius + 1, above[j * cb : (j + 1) * cb, :], sender)
            pre = grads[:, cols] + sender
            sig = sigmoid(pre)
            grads[:, cols] = sig * (1.0 + pre * (1.0 - sig))
            acc[...] += dot_nt(one_hot(node, half), upper_lower(upper, pre * sig))

    def nodes_of(out):
        out[:half, :] = acc[:, :cb].astype(bf16)
        out[half:, :] = acc[:, cb:].astype(bf16)

    def edges_backward(grad, src, dst, grads, back, rows_ref, out, inbound, tile):
        capacity, tiles = rows_ref.shape[1], src.shape[1] // tile
        acc[...] = jnp.zeros_like(acc)
        rows_ref[...] = jnp.zeros_like(rows_ref)
        copies = []

        def add_rows(slots, base, cols, d_pre):
            slot, low = slots_of(src[:, cols], capacity, offs)
            slot = slot.astype(jnp.int16)
            parts = [jnp.where(slot == j, d_pre, jnp.zeros((), bf16)) for j in slots]
            rows_ref[base : base + len(slots) * cb, :] += dot_nt(
                jnp.concatenate(parts, axis=0) if len(parts) > 1 else parts[0], one_hot(low, capacity)
            )

        for i, slots in enumerate(passes):
            base = 2 * i * cb

            @pl.loop(0, tiles)
            def _(t):
                cols = at(t, tile)
                if i == 0:
                    upper, node = halves_of(dst[:, cols], half)
                    d_pre = pick_half(upper, dot(grad, one_hot(node, half))) * grads[:, cols]
                    back[:, cols] = d_pre.astype(bf16)
                add_rows(slots, base, cols, back[:, cols])

            for n, j in enumerate(slots):
                out[j] = rows_ref[base + n * cb : base + (n + 1) * cb, :].astype(bf16)
            sends = [(out.at[j], inbound.at[j], {"band": band_at(radius - j)}) for j in slots]
            copies.append(send(sends, inbound.at[: len(slots)]))

        base = 2 * len(passes) * cb

        @pl.loop(0, tiles)
        def _(t):
            cols = at(t, tile)
            d_pre = back[:, cols]
            upper, node = halves_of(dst[:, cols], half)
            acc[...] += dot_nt(one_hot(node, half), upper_lower(upper, d_pre.astype(f32)))
            add_rows([radius], base, cols, d_pre)

        inbound[radius] = rows_ref[base : base + cb, :].astype(bf16)
        return copies

    tile_g = min(4096, g2m_src.shape[1])
    tile_m = min(4096, mesh_src.shape[1])
    arrive(mesh_copies)
    recv_g = two_rows(dot(wgr_t, mesh_full[...]).astype(bf16))
    edges_near(table, recv_g, wge_t, attr_g, g2m_src, g2m_dst, edge_grad, tile_g)
    m_relay = relay(group_m)
    arrive(halo)
    edges_far(table, g2m_src, g2m_dst, edge_grad, tile_g)
    nodes_of(nbuf)
    enc_copies = swap_rows(nbuf, enc_g)
    a_copies = share(fetched(group_a)[1])
    b_relay = relay(group_b)
    m_copies = relayed(m_relay)

    x = flip(mesh_full[:, at(c, nb)])
    arrive(gain_copies)
    gain_e = jnp.concatenate([gains[k, 0:1, :] for k in range(nchan)], axis=1)
    gain_p = jnp.concatenate([gains[k, 1:2, :] for k in range(nchan)], axis=1)
    arrive(a_copies)

    def mlp(pre, w_o):
        sig = sigmoid(pre)
        out = dot((pre * sig).astype(bf16), whole(w_o))
        normed, inverse = norm(out)
        return sig * (1.0 + pre * (1.0 - sig)), normed, inverse

    pre = dot(x.astype(bf16), whole(f_nm))
    arrive(enc_copies)
    enc_sg, enc_normed, enc_inverse = mlp(pre + dot(enc_g[...], whole(f_na)), f_no)
    mid = (x + enc_normed * gain_e).astype(bf16)
    arrive(m_copies)
    s_out[...] = dot(mid, whole(f_ms)).astype(bf16)
    s_copies = swap_lanes(s_out, s_in)
    r_out[...] = dot(mid, whole(f_mr)).astype(bf16)
    r_copies = swap_lanes(r_out, r_in)

    arrive(s_copies)
    mid_s[...] = flip(s_in[...]).astype(bf16)
    m_halo = pack(mid_s, mesh_send, m_halo_out, m_table)
    arrive(r_copies)
    c_relay = relay(group_c)
    cot_copies = to_chan(
        lambda p: cotangent.at[:, at(p, nb)], cot_rows.at[at(c, cb), :], cot_rows.at[: others * cb, :]
    )
    recv_m = two_rows(flip(r_in[...]).astype(bf16))
    edges_near(m_table, recv_m, wme_t, attr_m, mesh_src, mesh_dst, m_edge_grad, tile_m)
    arrive(m_halo)
    edges_far(m_table, mesh_src, mesh_dst, m_edge_grad, tile_m)
    nodes_of(m_nbuf)
    proc_copies = swap_rows(m_nbuf, proc_g)
    b_copies = relayed(b_relay)
    arrive(cot_copies)
    cot = flip(cot_rows[...])
    arrive(b_copies)
    pre = dot(mid, whole(f_pm))
    arrive(proc_copies)

    proc_sg, proc_normed, proc_inverse = mlp(pre + dot(proc_g[...], whole(f_pa)), f_po)
    d_out = norm_back(cot, proc_normed, proc_inverse, gain_p)
    d_hid = (dot_nt(d_out, whole(f_po)) * proc_sg).astype(bf16)
    dg_out[...] = dot_nt(whole(f_pa), d_hid).astype(bf16)
    dg_copies = swap_rows(dg_out, dg_in)
    c_copies = relayed(c_relay)
    mo_out[...] = flip(mid.astype(f32) + proc_normed * gain_p).astype(bf16)
    d_mid = cot + dot_nt(d_hid, whole(f_pm))
    arrive(dg_copies)
    mo_copies = swap_rows(mo_out, mo_in)
    m_back = edges_backward(
        two_rows(dg_in[...]), mesh_src, mesh_dst, m_edge_grad, m_edge_back,
        rows_acc, m_back_out, m_back_in, tile_m,
    )
    nodes_of(mr_out)
    mr_copies = swap_rows(mr_out, mr_in)

    def gather_back(copies, inbound, add):
        value = add(radius, inbound[radius])
        for slots, batch in zip(passes, copies):
            arrive(batch)
            for j in slots:
                value = value + add(j, inbound[j])
        return value

    h_out[...] = gather_back(
        m_back, m_back_in, lambda j, rows: dot_nt(one_hot(mesh_send[j : j + 1, :], mesh_dev), rows)
    ).astype(bf16)
    h_copies = swap_rows(h_out, h_in)
    arrive(mr_copies)
    d_mid = d_mid + dot_nt(mr_in[...], whole(f_mr))
    arrive(h_copies)
    d_mid = d_mid + dot_nt(h_in[...], whole(f_ms))

    d_out = norm_back(d_mid, enc_normed, enc_inverse, gain_e)
    d_hid = (dot_nt(d_out, whole(f_no)) * enc_sg).astype(bf16)
    de_out[...] = dot_nt(whole(f_na), d_hid).astype(bf16)
    de_copies = swap_rows(de_out, de_in)
    d_mesh = d_mid + dot_nt(d_hid, whole(f_nm))
    arrive(de_copies)

    g_back = edges_backward(
        two_rows(de_in[...]), g2m_src, g2m_dst, edge_grad, edge_back,
        g_rows_acc, g_back_out, g_back_in, tile_g,
    )
    nodes_of(er_out)
    er_copies = swap_rows(er_out, er_in)
    arrive(c_copies)
    dgrid_out[...] = gather_back(
        g_back, g_back_in, lambda j, rows: dot_nt(rows, one_hot(g2m_send[j : j + 1, :], grid_dev))
    ).astype(bf16)
    dgrid_copies = swap_lanes(dgrid_out, dgrid_in)
    arrive(er_copies)
    mg_out[...] = jnp.transpose(d_mesh + dot_nt(er_in[...], whole(f_gr)))
    arrive(dgrid_copies)
    dpre_out[...] = (dot(whole(f_gs), dgrid_in[...]) * sgrid[:, at(c, gb)]).astype(bf16)
    dpre_copies = swap_rows(dpre_out, dpre_in)
    arrive(mo_copies)
    mesh_out[...] = mo_in[...]
    arrive(dpre_copies)

    share_rows, piece = part.shape[0] // 2, part.shape[0] // inner
    part[at(1 - core, share_rows), :] = dot_nt(gpad[at(1 - core, share_rows), :], dpre_in[...]).astype(bf16)
    pair = send([(part.at[at(1 - core, share_rows), :], pair_in, {"band": sibling})], pair_in)
    mg_copies = swap_rows(mg_out, mg_in)
    mine_half = dot_nt(gpad[at(core, share_rows), :], dpre_in[...])
    arrive(pair)
    pair_sum[...] = (mine_half + pair_in[...].astype(f32)).astype(bf16)
    first = send(
        [(pair_sum.at[at(p, piece), :], rs1.at[row], {"band": b}) for p, b in zip(row_peers, inner_peers)],
        rs1.at[: rows - 1],
    )
    rs1[row] = pair_sum[at(row, piece), :]
    arrive(first)
    mine[...] = jnp.sum(rs1[...].astype(f32), axis=0)
    second = send([(mine, rs2.at[group], {"band": b}) for b in outer_peers], rs2.at[: outer - 1])
    rs2[group] = mine[...]
    arrive(mg_copies)
    mesh_grad[...] = mg_in[...]
    arrive(second)
    own = at(core * rows + row, piece)
    total[own, :] = (jnp.sum(rs2[...], axis=0) * scale).astype(bf16)
    third = send([(total.at[own, :], total.at[own, :], {"band": b}) for b in inner_peers], total.at[: (rows - 1) * piece, :])
    arrive(third)
    done = total.at[at(core, share_rows), :]
    arrive(send([(done, done, {"band": sibling})], done))
    w_grid_sum[...] = total[...]
    for batch in list(started):
        sent(batch)


def hand_over(mesh_out_in, mesh_grad_in, w_grid_sum, mesh_out, mesh_grad, w_grid_grad):
    mesh_out[...] = mesh_out_in[...]
    mesh_grad[...] = mesh_grad_in[...]
    w_grid_grad[...] = w_grid_sum[0 : w_grid_grad.shape[0], :].astype(f32)


def local(nband, nchan, inner, *args):
    names = INPUTS
    a = dict(zip(names, args))
    for name in ("g2m_src", "g2m_dst", "mesh_src", "mesh_dst", "gain_enc", "gain_proc"):
        a[name] = a[name].reshape(1, -1)
    fin, grid_dev = a["grid_in"].shape
    width, cb = a["w_gs"].shape
    mesh_dev = a["mesh_in"].shape[1]
    nb, gb = mesh_dev // nchan, grid_dev // nchan
    offs, cap = a["g2m_send"].shape
    mcap = a["mesh_send"].shape[1]
    edges, medges = a["g2m_src"].shape[1], a["mesh_src"].shape[1]
    fp = -(-fin // 128) * 128
    scale = float(grid_dev * nband) ** (-0.5)
    v = pltpu.VMEM
    nodes = v((mesh_dev, cb), bf16)
    block = v((nb, width), bf16)
    held = [
        *("grid_in", "w_grid", "g2m_attr", "g2m_send", "g2m_src", "g2m_dst", "w_gs", "w_gr", "w_ge", "gain_enc"),
        *("mesh_attr", "mesh_send", "mesh_src", "mesh_dst", "w_me", "gain_proc"),
    ]
    scratch = [
        *[v(a[name].shape, a[name].dtype) for name in held],
        v((fp, grid_dev), bf16), v((fp, cb), bf16), v((width, fp), bf16), v((16, cb), f32),
        v((16, edges), bf16), v((16, medges), bf16),
        v((width, mesh_dev), bf16), v((nchan, 8, cb), f32), v((width, nb), bf16),
        v((10, nchan, cb, width), bf16),
        v((width, grid_dev), f32), v((cb, grid_dev), bf16), v((offs, cb, cap), bf16), v((offs * cb, cap), bf16),
        v((cb, edges), f32), v((cb, edges), bf16),
        v((mesh_dev // 2, 2 * cb), f32), nodes, block,
        block, block, nodes, nodes, v((cb, mesh_dev), bf16), v((offs, cb, mcap), bf16), v((offs * cb, mcap), bf16),
        v((cb, medges), f32), v((cb, medges), bf16), nodes, block,
        *[v((width, nb), bf16), v((cb, mesh_dev), bf16)] * 2, v((offs * cb, mcap), f32),
        v((offs, cb, mcap), bf16), v((offs, cb, mcap), bf16), nodes, block, nodes, block,
        v((width, nb), bf16), v((cb, mesh_dev), bf16), v((offs * cb, cap), f32), v((offs, cb, cap), bf16), v((offs, cb, cap), bf16), nodes, block,
        v((width, nb), f32), v((cb, mesh_dev), f32),
        v((cb, grid_dev), bf16), v((width, gb), bf16), v((width, gb), bf16), v((cb, grid_dev), bf16),
        v((fp, cb), bf16), v((fp // 2, cb), bf16), v((fp // 2, cb), bf16), v((inner // 2, fp // inner, cb), bf16),
        v((fp // inner, cb), f32), v((nband // inner, fp // inner, cb), f32), v((fp, cb), bf16),
        pltpu.SemaphoreType.DMA((BATCHES,)), pltpu.SemaphoreType.DMA((BATCHES,)), pltpu.SemaphoreType.DMA((OWN,)),
    ]
    spec, anywhere = pl.BlockSpec(memory_space=pltpu.VMEM), pl.BlockSpec(memory_space=pl.ANY)
    results = pl.pallas_call(
        functools.partial(kernel, nband, nchan, inner, scale),
        out_shape=(
            jax.ShapeDtypeStruct((cb, mesh_dev), bf16),
            jax.ShapeDtypeStruct((cb, mesh_dev), f32),
            jax.ShapeDtypeStruct((fp, cb), bf16),
        ),
        in_specs=[anywhere] * len(names),
        out_specs=(spec,) * 3,
        scratch_shapes=scratch,
        compiler_params=pltpu.CompilerParams(
            collective_id=0, has_side_effects=True, vmem_limit_bytes=56 * 2**20
        ),
    )(*[a[name] for name in names])
    return pl.pallas_call(
        hand_over,
        out_shape=(
            jax.ShapeDtypeStruct((cb, mesh_dev), bf16),
            jax.ShapeDtypeStruct((cb, mesh_dev), f32),
            jax.ShapeDtypeStruct((fin, cb), f32),
        ),
        in_specs=[spec] * 3,
        out_specs=(spec,) * 3,
    )(*results)


def solution(mesh):
    nband, nchan = mesh.shape["band"], mesh.shape["chan"]
    inner = min(16, nband // 2)
    return jax.shard_map(
        functools.partial(local, nband, nchan, inner),
        mesh=mesh,
        in_specs=(
            P(None, "band"),
            P(None, "chan"),
            P("chan", "band"),
            P(None, "band"),
            P("band", None),
            P("band"),
            P("band"),
            P(None, "chan"),
            P(None, "chan"),
            P(None, "chan"),
            P("chan", None),
            P("chan", None),
            P("chan", None),
            P("chan"),
            P(None, "band"),
            P("band", None),
            P("band"),
            P("band"),
            P(None, "chan"),
            P(None, "chan"),
            P(None, "chan"),
            P("chan", None),
            P("chan", None),
            P("chan", None),
            P("chan"),
            P("chan", "band"),
        ),
        out_specs=(P("chan", "band"), P("chan", "band"), P(None, "chan")),
        check_vma=False,
    )
```

```python
import functools

import jax
import jax.numpy as jnp
from jax import lax
from jax.experimental import pallas as pl
from jax.experimental.pallas import tpu as pltpu
from jax.sharding import PartitionSpec as P

eps = 1e-05
bf16 = jnp.bfloat16
f32 = jnp.float32
MESH = pl.DeviceIdType.MESH
BATCHES, OWN = 42, 25
INPUTS = (
    *("grid_in", "w_grid", "mesh_in", "g2m_attr", "g2m_send", "g2m_src", "g2m_dst"),
    *("w_gs", "w_gr", "w_ge", "w_nm", "w_na", "w_no", "gain_enc"),
    *("mesh_attr", "mesh_send", "mesh_src", "mesh_dst"),
    *("w_ms", "w_mr", "w_me", "w_pm", "w_pa", "w_po", "gain_proc", "cotangent"),
)


def whole(f):
    return f[...].reshape(f.shape[0] * f.shape[1], f.shape[2])


def dot(a, b):
    return jnp.dot(a, b, preferred_element_type=f32)


def dot_nt(a, b):
    return lax.dot_general(a, b, (((1,), (1,)), ((), ())), preferred_element_type=f32)


def flip(x):
    return jnp.transpose(x.astype(f32))


def sigmoid(v):
    return 0.5 + 0.5 * jnp.tanh(0.5 * v)


def one_hot(ids, count):
    rows = lax.broadcasted_iota(jnp.int16, (count, ids.shape[1]), 0)
    return jnp.where(rows == ids.astype(jnp.int16), jnp.ones((), bf16), jnp.zeros((), bf16))


def slots_of(ids, capacity, slots):
    slot = jnp.zeros_like(ids)
    for j in range(1, slots):
        slot = slot + (ids >= j * capacity).astype(jnp.int32)
    return slot, ids - slot * capacity


def halves_of(ids, half):
    upper = ids >= half
    return upper, jnp.where(upper, ids - half, ids)


def two_rows(x):
    half = x.shape[1] // 2
    return jnp.concatenate([x[:, :half], x[:, half:]], axis=0)


def norm(out):
    width = out.shape[1]
    mean = jnp.sum(out, axis=1, keepdims=True) / width
    var = jnp.sum(out * out, axis=1, keepdims=True) / width - mean * mean
    inverse = lax.rsqrt(var + eps)
    return (out - mean) * inverse, inverse


def norm_back(grad, normed, inverse, gain):
    width = grad.shape[1]
    u = grad * gain
    a = jnp.sum(u, axis=1, keepdims=True) / width
    b = jnp.sum(u * normed, axis=1, keepdims=True) / width
    return ((u - a - normed * b) * inverse).astype(bf16)


def kernel(
    nband, nchan, inner, scale,
    grid_hbm, w_grid_hbm, mesh_in, g2m_attr_hbm, g2m_send_hbm, g2m_src_hbm, g2m_dst_hbm,
    w_gs_hbm, w_gr_hbm, w_ge_hbm, w_nm, w_na, w_no, gain_enc_hbm,
    mesh_attr_hbm, mesh_send_hbm, mesh_src_hbm, mesh_dst_hbm,
    w_ms, w_mr, w_me_hbm, w_pm, w_pa, w_po, gain_proc_hbm, cotangent,
    mesh_out, mesh_grad, w_grid_sum,
    grid_in, w_grid, g2m_attr, g2m_send, g2m_src, g2m_dst, w_gs, w_gr, w_ge, gain_enc,
    mesh_attr, mesh_send, mesh_src, mesh_dst, w_me, gain_proc,
    gpad, wg_pad, wg_t, we_pad, attr_g, attr_m,
    mesh_full, gains, cot_rows,
    f_all,
    sgrid, s_grid, halo_out, table, edge_grad, edge_back,
    acc, nbuf, enc_g,
    s_out, r_out, s_in, r_in, mid_s, m_halo_out, m_table, m_edge_grad, m_edge_back, m_nbuf, proc_g,
    mo_out, mo_in, dg_out, dg_in, rows_acc, m_back_out, m_back_in, mr_out, mr_in, h_out, h_in,
    de_out, de_in, g_rows_acc, g_back_out, g_back_in, er_out, er_in, mg_out, mg_in,
    dgrid_out, dgrid_in, dpre_out, dpre_in,
    part, pair_in, pair_sum, rs1, mine, rs2, total,
    ssem, rsem, lsem,
):
    d, c = lax.axis_index("band"), lax.axis_index("chan")
    core = lax.rem(d, 2)
    sibling = d + 1 - 2 * core
    width, cb = w_gs.shape
    fin, grid_dev = grid_in.shape
    mesh_dev = mesh_in.shape[1]
    nb = mesh_dev // nchan
    gb = grid_dev // nchan
    half = mesh_dev // 2
    offs, cap = g2m_send.shape
    radius = offs // 2
    ea = w_ge.shape[0]
    f_nm, f_na, f_no, f_ms, f_mr, f_pm, f_pa, f_po, f_gs, f_gr = (
        f_all.at[i] for i in range(10)
    )
    count = [0]
    local_count = [0]
    started = []

    def at(index, size):
        return pl.ds(pl.multiple_of(index * size, size), size)

    def fetch_local(src, dst):
        copy = pltpu.make_async_copy(src, dst, lsem.at[local_count[0]])
        local_count[0] += 1
        copy.start()
        return copy

    def wait_on(whole, i):
        return pltpu.make_async_remote_copy(
            src_ref=whole, dst_ref=whole, send_sem=ssem.at[i], recv_sem=rsem.at[i],
            device_id={"band": sibling}, device_id_type=MESH,
        )

    def send(sends, whole):
        i = count[0]
        count[0] += 1
        for src, dst, target in sends:
            pltpu.make_async_remote_copy(
                src_ref=src, dst_ref=dst, send_sem=ssem.at[i], recv_sem=rsem.at[i],
                device_id=target, device_id_type=MESH,
            ).start()
        batch = (whole, i)
        started.append(batch)
        return batch

    def sent(batch):
        wait_on(*batch).wait_send()
        started[:] = [other for other in started if other is not batch]

    def arrive(batch):
        wait_on(*batch).wait_recv()

    own_w_grid = fetch_local(w_grid_hbm, w_grid)
    own_w_gs = fetch_local(w_gs_hbm, w_gs)
    own_grid = fetch_local(grid_hbm, grid_in)
    own_mesh = fetch_local(mesh_in, mesh_full.at[at(c, cb), :])
    own_rest = [
        fetch_local(src, dst)
        for src, dst in (
            (g2m_send_hbm, g2m_send), (w_gr_hbm, w_gr), (w_ge_hbm, w_ge), (g2m_attr_hbm, g2m_attr),
            (g2m_src_hbm, g2m_src), (g2m_dst_hbm, g2m_dst), (gain_enc_hbm, gain_enc), (gain_proc_hbm, gain_proc),
            (mesh_attr_hbm, mesh_attr), (mesh_send_hbm, mesh_send), (mesh_src_hbm, mesh_src),
            (mesh_dst_hbm, mesh_dst), (w_me_hbm, w_me), (cotangent.at[:, at(c, nb)], cot_rows.at[at(c, cb), :]),
        )
    ]

    def far_first(size):
        return sorted(range(1, size), key=lambda k: -min(k, size - k))

    chan_peers = [lax.rem(c + k, nchan) for k in far_first(nchan)]

    def band_at(offset):
        return lax.rem(d + offset + nband, nband)

    near = [band_at(o) for o in range(-radius, radius + 1) if o != 0]
    group, place = d // inner, lax.rem(d, inner)
    row, rows = place // 2, inner // 2
    row_peers = [lax.rem(row + k, rows) for k in far_first(rows)]
    inner_peers = [group * inner + 2 * p + core for p in row_peers]
    outer = nband // inner
    outer_peers = [lax.rem(group + k, outer) * inner + place for k in far_first(outer)]
    met = near + inner_peers + outer_peers + [sibling]
    barrier = pltpu.get_barrier_semaphore()
    for p in chan_peers:
        pl.semaphore_signal(barrier, inc=1, device_id={"chan": p}, device_id_type=MESH)
    for b in met:
        pl.semaphore_signal(barrier, inc=1, device_id={"band": b}, device_id_type=MESH)

    others = nchan - 1

    def to_chan(src_of, dst, whole):
        return send([(src_of(p), dst, {"chan": p}) for p in chan_peers], whole)

    def swap_rows(src, dst):
        size, lanes = dst.shape[0], src.shape[1]
        batch = to_chan(lambda p: src.at[at(p, size), :], dst.at[:, at(c, lanes)], dst.at[:, : others * lanes])
        dst[:, at(c, lanes)] = src[at(c, size), :]
        return batch

    def swap_lanes(src, dst):
        size, lanes = src.shape[0], dst.shape[1]
        batch = to_chan(lambda p: src.at[:, at(p, lanes)], dst.at[at(c, size), :], dst.at[: others * size, :])
        dst[at(c, size), :] = src[:, at(c, lanes)]
        return batch

    tail = fin // 16 * 16
    wg_pad[tail:, :] = jnp.zeros((wg_pad.shape[0] - tail, cb), bf16)
    own_w_grid.wait()
    wg_pad[0:fin, :] = w_grid[...]
    wg_t[at(c, cb), :] = flip(wg_pad[...]).astype(bf16)
    pl.semaphore_wait(barrier, len(chan_peers) + len(met))

    def wg_half(p):
        return wg_t.at[at(2 * p + core, cb // 2), :]

    wg_copies = [send([(wg_half(c), wg_half(c), {"chan": p})], wg_half(c)) for p in chan_peers]
    gains[c] = jnp.zeros(gains.shape[1:], f32)

    gpad[tail:, :] = jnp.zeros((gpad.shape[0] - tail, grid_dev), bf16)
    own_grid.wait()
    gpad[0:fin, :] = grid_in[...]
    own_w_gs.wait()
    wgs_t = flip(w_gs[...]).astype(bf16)
    own_mesh.wait()
    for copy in own_rest:
        copy.wait()
    for batch in wg_copies:
        sent(batch)
    mesh_copies = to_chan(lambda p: mesh_in, mesh_full.at[at(c, cb), :], mesh_full.at[: others * cb, :])
    gains[c, 0:1, :] = gain_enc[...]
    gains[c, 1:2, :] = gain_proc[...]
    we_pad[...] = jnp.zeros_like(we_pad)
    we_pad[0:ea, :] = w_ge[...].astype(f32)
    wge_t = jnp.transpose(we_pad[...]).astype(bf16)
    we_pad[0:ea, :] = w_me[...].astype(f32)
    wme_t = jnp.transpose(we_pad[...]).astype(bf16)
    attr_g[...] = jnp.zeros_like(attr_g)
    attr_g[0:ea, :] = g2m_attr[...]
    attr_m[...] = jnp.zeros_like(attr_m)
    attr_m[0:ea, :] = mesh_attr[...]
    wgr_t = flip(w_gr[...]).astype(bf16)

    def passed_on():
        for batch, k in zip(wg_copies, far_first(nchan)[::-1]):
            arrive(batch)
            piece = wg_half(lax.rem(c - k + nchan, nchan))
            yield piece, piece, {"band": sibling}


    wg_copies.reverse()
    wg_shared = send(passed_on(), wg_t.at[: others * cb // 2, :])

    def part_of(shard, full, cuts):
        index = group if cuts > 1 else 0
        if shard.shape[0] == cb:
            rows, lanes = at(index, cb // cuts), at(core, width // 2)
            return shard.at[rows, lanes], full.at[c, rows, lanes], full.at[:, rows, lanes], full.at[:, :, lanes]
        blocks = at(core, nchan // 2)
        size = width // 2 // cuts
        if size >= cb:
            blocks, rows = at(core * cuts + index, size // cb), pl.ds(0, cb)
        else:
            first = (core * cuts + index) * size
            blocks, rows = pl.ds(first // cb, 1), pl.ds(pl.multiple_of(lax.rem(first, cb), size), size)
        source = shard.at[at(core * cuts + index, size), :]
        if size >= cb:
            source = [shard.at[at((core * cuts + index) * (size // cb) + n, cb), :] for n in range(size // cb)]
            target = [full.at[(core * cuts + index) * (size // cb) + n, :, at(c, cb)] for n in range(size // cb)]
        else:
            source, target = [source], [full.at[first // cb, rows, at(c, cb)]]
        return source, target, full.at[blocks, rows, :], full.at[at(core, nchan // 2), :, :]

    def listed(x):
        return x if isinstance(x, list) else [x]

    def fetch(pairs, cuts=1):
        sends, regions, halves, own = [], [], [], local_count[0]
        local_count[0] += 1
        for shard, full in pairs:
            src, dst, region, whole = part_of(shard, full, cuts)
            for one, other in zip(listed(src), listed(dst)):
                pltpu.make_async_copy(one, other, lsem.at[own]).start()
                sends += [(one, other, {"chan": p}) for p in chan_peers]
            regions.append(region)
            halves.append(whole)
        unit = cb // 2 // cuts
        size = len(pairs)
        return send(sends, f_all.at[:size, :others, :unit, :]), own, f_all.at[:size, 0, :unit, :], regions, halves

    def fetched(group_copies):
        inbound, own, own_whole, regions, halves = group_copies
        pltpu.make_async_copy(own_whole, own_whole, lsem.at[own]).wait()
        arrive(inbound)
        return regions, halves

    def relay(group_copies):
        regions, halves = fetched(group_copies)
        sends = [(r, r, {"band": b}) for r in regions for b in outer_peers]
        unit = nchan * cb // 2 // outer
        return send(sends, f_all.at[: len(regions), : outer - 1, :unit, :]), halves

    def share(halves):
        return send([(w, w, {"band": sibling}) for w in halves], f_all.at[: len(halves), : nchan // 2, :, :])

    def relayed(relay_copies):
        arrive(relay_copies[0])
        return share(relay_copies[1])

    sent(mesh_copies)
    gain_copies = to_chan(lambda p: gains.at[c], gains.at[c], gains.at[:others])
    group_m = fetch([(w_ms, f_ms), (w_mr, f_mr)], outer)
    group_a = fetch([(w_nm, f_nm), (w_na, f_na), (w_no, f_no)])

    arrive(wg_shared)

    step = min(512, grid_dev)

    @pl.loop(0, grid_dev // step)
    def _(t):
        cols = at(t, step)
        pre = dot(wg_t[...], gpad[:, cols])
        sig = sigmoid(pre)
        sgrid[:, cols] = sig * (1.0 + pre * (1.0 - sig))
        s_grid[:, cols] = dot(wgs_t, (pre * sig).astype(bf16)).astype(bf16)

    order = [j for o in range(radius, 0, -1) for j in (radius - o, radius + o)]
    passes = [order[i : i + 2] for i in range(0, len(order), 2)]

    def pack(field, lists, out, dest):
        def picked(j):
            return dot(field[...], one_hot(lists[j : j + 1, :], field.shape[1])).astype(bf16)

        def block(n):
            return dest.at[n * cb : (n + 1) * cb, :]

        def sends():
            for n, j in enumerate(order):
                out[j] = picked(j)
                yield out.at[j], block(n), {"band": band_at(j - radius)}

        batch = send(sends(), dest.at[: (offs - 1) * cb, :])
        dest[len(order) * cb :, :] = picked(radius)
        return batch

    halo = pack(s_grid, g2m_send, halo_out, table)

    group_b = fetch([(w_pm, f_pm), (w_pa, f_pa), (w_po, f_po)], outer)
    group_c = fetch([(w_gr, f_gr), (w_gs, f_gs)], outer)

    def upper_lower(upper, x):
        return jnp.concatenate([jnp.where(upper, 0.0, x), jnp.where(upper, x, 0.0)], axis=0).astype(bf16)

    def pick_half(upper, pair):
        return jnp.where(upper, pair[cb:], pair[:cb])

    def edges_near(table, recv, w_edge_t, attr, src, dst, grads, tile):
        @pl.loop(0, src.shape[1] // tile)
        def _(t):
            cols = at(t, tile)
            slot, low = slots_of(src[:, cols], table.shape[1], offs)
            upper, node = halves_of(dst[:, cols], half)
            own = dot(table[len(order) * cb :, :], one_hot(low, table.shape[1]))
            pre = jnp.where(slot == radius, own, 0.0) + dot(w_edge_t, attr[:, cols])
            grads[:, cols] = pre + pick_half(upper, dot(recv, one_hot(node, half)))

    def edges_far(table, src, dst, grads, tile):
        acc[...] = jnp.zeros_like(acc)

        @pl.loop(0, src.shape[1] // tile)
        def _(t):
            cols = at(t, tile)
            slot, low = slots_of(src[:, cols], table.shape[1], offs)
            upper, node = halves_of(dst[:, cols], half)
            remote = dot(table[: len(order) * cb, :], one_hot(low, table.shape[1]))
            sender = jnp.zeros((cb, tile), f32)
            for n, j in enumerate(order):
                sender = jnp.where(slot == j, remote[n * cb : (n + 1) * cb, :], sender)
            pre = grads[:, cols] + sender
            sig = sigmoid(pre)
            grads[:, cols] = sig * (1.0 + pre * (1.0 - sig))
            acc[...] += dot_nt(one_hot(node, half), upper_lower(upper, pre * sig))

    def nodes_of(out):
        out[:half, :] = acc[:, :cb].astype(bf16)
        out[half:, :] = acc[:, cb:].astype(bf16)

    def edges_backward(grad, src, dst, grads, back, rows_ref, out, inbound, tile):
        capacity, tiles = rows_ref.shape[1], src.shape[1] // tile
        acc[...] = jnp.zeros_like(acc)
        rows_ref[...] = jnp.zeros_like(rows_ref)
        copies = []

        def add_rows(slots, base, cols, d_pre):
            slot, low = slots_of(src[:, cols], capacity, offs)
            slot = slot.astype(jnp.int16)
            parts = [jnp.where(slot == j, d_pre, jnp.zeros((), bf16)) for j in slots]
            rows_ref[base : base + len(slots) * cb, :] += dot_nt(
                jnp.concatenate(parts, axis=0) if len(parts) > 1 else parts[0], one_hot(low, capacity)
            )

        for i, slots in enumerate(passes):
            base = 2 * i * cb

            @pl.loop(0, tiles)
            def _(t):
                cols = at(t, tile)
                if i == 0:
                    upper, node = halves_of(dst[:, cols], half)
                    d_pre = pick_half(upper, dot(grad, one_hot(node, half))) * grads[:, cols]
                    back[:, cols] = d_pre.astype(bf16)
                add_rows(slots, base, cols, back[:, cols])

            for n, j in enumerate(slots):
                out[j] = rows_ref[base + n * cb : base + (n + 1) * cb, :].astype(bf16)
            sends = [(out.at[j], inbound.at[j], {"band": band_at(radius - j)}) for j in slots]
            copies.append(send(sends, inbound.at[: len(slots)]))

        base = 2 * len(passes) * cb

        @pl.loop(0, tiles)
        def _(t):
            cols = at(t, tile)
            d_pre = back[:, cols]
            upper, node = halves_of(dst[:, cols], half)
            acc[...] += dot_nt(one_hot(node, half), upper_lower(upper, d_pre.astype(f32)))
            add_rows([radius], base, cols, d_pre)

        inbound[radius] = rows_ref[base : base + cb, :].astype(bf16)
        return copies

    tile_g = min(4096, g2m_src.shape[1])
    tile_m = min(4096, mesh_src.shape[1])
    arrive(mesh_copies)
    recv_g = two_rows(dot(wgr_t, mesh_full[...]).astype(bf16))
    edges_near(table, recv_g, wge_t, attr_g, g2m_src, g2m_dst, edge_grad, tile_g)
    m_relay = relay(group_m)
    arrive(halo)
    edges_far(table, g2m_src, g2m_dst, edge_grad, tile_g)
    nodes_of(nbuf)
    enc_copies = swap_rows(nbuf, enc_g)
    a_copies = share(fetched(group_a)[1])
    b_relay = relay(group_b)
    m_copies = relayed(m_relay)

    x = flip(mesh_full[:, at(c, nb)])
    arrive(gain_copies)
    gain_e = jnp.concatenate([gains[k, 0:1, :] for k in range(nchan)], axis=1)
    gain_p = jnp.concatenate([gains[k, 1:2, :] for k in range(nchan)], axis=1)
    arrive(a_copies)

    def mlp(pre, w_o):
        sig = sigmoid(pre)
        out = dot((pre * sig).astype(bf16), whole(w_o))
        normed, inverse = norm(out)
        return sig * (1.0 + pre * (1.0 - sig)), normed, inverse

    pre = dot(x.astype(bf16), whole(f_nm))
    arrive(enc_copies)
    enc_sg, enc_normed, enc_inverse = mlp(pre + dot(enc_g[...], whole(f_na)), f_no)
    mid = (x + enc_normed * gain_e).astype(bf16)
    arrive(m_copies)
    s_out[...] = dot(mid, whole(f_ms)).astype(bf16)
    s_copies = swap_lanes(s_out, s_in)
    r_out[...] = dot(mid, whole(f_mr)).astype(bf16)
    r_copies = swap_lanes(r_out, r_in)

    arrive(s_copies)
    mid_s[...] = flip(s_in[...]).astype(bf16)
    m_halo = pack(mid_s, mesh_send, m_halo_out, m_table)
    arrive(r_copies)
    c_relay = relay(group_c)
    cot_copies = to_chan(
        lambda p: cotangent.at[:, at(p, nb)], cot_rows.at[at(c, cb), :], cot_rows.at[: others * cb, :]
    )
    recv_m = two_rows(flip(r_in[...]).astype(bf16))
    edges_near(m_table, recv_m, wme_t, attr_m, mesh_src, mesh_dst, m_edge_grad, tile_m)
    arrive(m_halo)
    edges_far(m_table, mesh_src, mesh_dst, m_edge_grad, tile_m)
    nodes_of(m_nbuf)
    proc_copies = swap_rows(m_nbuf, proc_g)
    b_copies = relayed(b_relay)
    arrive(cot_copies)
    cot = flip(cot_rows[...])
    arrive(b_copies)
    pre = dot(mid, whole(f_pm))
    arrive(proc_copies)

    proc_sg, proc_normed, proc_inverse = mlp(pre + dot(proc_g[...], whole(f_pa)), f_po)
    d_out = norm_back(cot, proc_normed, proc_inverse, gain_p)
    d_hid = (dot_nt(d_out, whole(f_po)) * proc_sg).astype(bf16)
    dg_out[...] = dot_nt(whole(f_pa), d_hid).astype(bf16)
    dg_copies = swap_rows(dg_out, dg_in)
    c_copies = relayed(c_relay)
    mo_out[...] = flip(mid.astype(f32) + proc_normed * gain_p).astype(bf16)
    d_mid = cot + dot_nt(d_hid, whole(f_pm))
    arrive(dg_copies)
    mo_copies = swap_rows(mo_out, mo_in)
    m_back = edges_backward(
        two_rows(dg_in[...]), mesh_src, mesh_dst, m_edge_grad, m_edge_back,
        rows_acc, m_back_out, m_back_in, tile_m,
    )
    nodes_of(mr_out)
    mr_copies = swap_rows(mr_out, mr_in)

    def gather_back(copies, inbound, add):
        value = add(radius, inbound[radius])
        for slots, batch in zip(passes, copies):
            arrive(batch)
            for j in slots:
                value = value + add(j, inbound[j])
        return value

    h_out[...] = gather_back(
        m_back, m_back_in, lambda j, rows: dot_nt(one_hot(mesh_send[j : j + 1, :], mesh_dev), rows)
    ).astype(bf16)
    h_copies = swap_rows(h_out, h_in)
    arrive(mr_copies)
    d_mid = d_mid + dot_nt(mr_in[...], whole(f_mr))
    arrive(h_copies)
    d_mid = d_mid + dot_nt(h_in[...], whole(f_ms))

    d_out = norm_back(d_mid, enc_normed, enc_inverse, gain_e)
    d_hid = (dot_nt(d_out, whole(f_no)) * enc_sg).astype(bf16)
    de_out[...] = dot_nt(whole(f_na), d_hid).astype(bf16)
    de_copies = swap_rows(de_out, de_in)
    d_mesh = d_mid + dot_nt(d_hid, whole(f_nm))
    arrive(de_copies)

    g_back = edges_backward(
        two_rows(de_in[...]), g2m_src, g2m_dst, edge_grad, edge_back,
        g_rows_acc, g_back_out, g_back_in, tile_g,
    )
    nodes_of(er_out)
    er_copies = swap_rows(er_out, er_in)
    arrive(c_copies)
    dgrid_out[...] = gather_back(
        g_back, g_back_in, lambda j, rows: dot_nt(rows, one_hot(g2m_send[j : j + 1, :], grid_dev))
    ).astype(bf16)
    dgrid_copies = swap_lanes(dgrid_out, dgrid_in)
    arrive(er_copies)
    mg_out[...] = jnp.transpose(d_mesh + dot_nt(er_in[...], whole(f_gr)))
    arrive(dgrid_copies)
    dpre_out[...] = (dot(whole(f_gs), dgrid_in[...]) * sgrid[:, at(c, gb)]).astype(bf16)
    dpre_copies = swap_rows(dpre_out, dpre_in)
    arrive(mo_copies)
    outputs = [fetch_local(mo_in, mesh_out)]
    arrive(dpre_copies)

    share_rows, piece = part.shape[0] // 2, part.shape[0] // inner
    part[at(1 - core, share_rows), :] = dot_nt(gpad[at(1 - core, share_rows), :], dpre_in[...]).astype(bf16)
    pair = send([(part.at[at(1 - core, share_rows), :], pair_in, {"band": sibling})], pair_in)
    mg_copies = swap_rows(mg_out, mg_in)
    mine_half = dot_nt(gpad[at(core, share_rows), :], dpre_in[...])
    arrive(pair)
    pair_sum[...] = (mine_half + pair_in[...].astype(f32)).astype(bf16)
    first = send(
        [(pair_sum.at[at(p, piece), :], rs1.at[row], {"band": b}) for p, b in zip(row_peers, inner_peers)],
        rs1.at[: rows - 1],
    )
    rs1[row] = pair_sum[at(row, piece), :]
    arrive(first)
    mine[...] = jnp.sum(rs1[...].astype(f32), axis=0)
    second = send([(mine, rs2.at[group], {"band": b}) for b in outer_peers], rs2.at[: outer - 1])
    rs2[group] = mine[...]
    arrive(mg_copies)
    outputs.append(fetch_local(mg_in, mesh_grad))
    arrive(second)
    own = at(core * rows + row, piece)
    total[own, :] = (jnp.sum(rs2[...], axis=0) * scale).astype(bf16)
    third = send([(total.at[own, :], total.at[own, :], {"band": b}) for b in inner_peers], total.at[: (rows - 1) * piece, :])
    arrive(third)
    done = total.at[at(core, share_rows), :]
    arrive(send([(done, done, {"band": sibling})], done))
    outputs.append(fetch_local(total, w_grid_sum))
    for batch in list(started):
        sent(batch)
    for copy in outputs:
        copy.wait()


def hand_over(
    mesh_out_in, mesh_grad_in, w_grid_sum, mesh_out, mesh_grad, w_grid_grad,
    held_out, held_grad, held_sum, held_w, sems,
):
    def copy(i, src, dst):
        started = pltpu.make_async_copy(src, dst, sems.at[i])
        started.start()
        return started

    grad_in = copy(0, mesh_grad_in, held_grad)
    sum_in = copy(1, w_grid_sum, held_sum)
    out_in = copy(2, mesh_out_in, held_out)
    grad_in.wait()
    grad_out = copy(3, held_grad, mesh_grad)
    sum_in.wait()
    held_w[...] = held_sum[0 : held_w.shape[0], :].astype(f32)
    w_out = copy(4, held_w, w_grid_grad)
    out_in.wait()
    out_out = copy(5, held_out, mesh_out)
    for last in (grad_out, w_out, out_out):
        last.wait()


def local(nband, nchan, inner, *args):
    names = INPUTS
    a = dict(zip(names, args))
    for name in ("g2m_src", "g2m_dst", "mesh_src", "mesh_dst", "gain_enc", "gain_proc"):
        a[name] = a[name].reshape(1, -1)
    fin, grid_dev = a["grid_in"].shape
    width, cb = a["w_gs"].shape
    mesh_dev = a["mesh_in"].shape[1]
    nb, gb = mesh_dev // nchan, grid_dev // nchan
    offs, cap = a["g2m_send"].shape
    mcap = a["mesh_send"].shape[1]
    edges, medges = a["g2m_src"].shape[1], a["mesh_src"].shape[1]
    fp = -(-fin // 128) * 128
    scale = float(grid_dev * nband) ** (-0.5)
    v = pltpu.VMEM
    nodes = v((mesh_dev, cb), bf16)
    block = v((nb, width), bf16)
    held = [
        *("grid_in", "w_grid", "g2m_attr", "g2m_send", "g2m_src", "g2m_dst", "w_gs", "w_gr", "w_ge", "gain_enc"),
        *("mesh_attr", "mesh_send", "mesh_src", "mesh_dst", "w_me", "gain_proc"),
    ]
    scratch = [
        *[v(a[name].shape, a[name].dtype) for name in held],
        v((fp, grid_dev), bf16), v((fp, cb), bf16), v((width, fp), bf16), v((16, cb), f32),
        v((16, edges), bf16), v((16, medges), bf16),
        v((width, mesh_dev), bf16), v((nchan, 8, cb), f32), v((width, nb), bf16),
        v((10, nchan, cb, width), bf16),
        v((width, grid_dev), f32), v((cb, grid_dev), bf16), v((offs, cb, cap), bf16), v((offs * cb, cap), bf16),
        v((cb, edges), f32), v((cb, edges), bf16),
        v((mesh_dev // 2, 2 * cb), f32), nodes, block,
        block, block, nodes, nodes, v((cb, mesh_dev), bf16), v((offs, cb, mcap), bf16), v((offs * cb, mcap), bf16),
        v((cb, medges), f32), v((cb, medges), bf16), nodes, block,
        *[v((width, nb), bf16), v((cb, mesh_dev), bf16)] * 2, v((offs * cb, mcap), f32),
        v((offs, cb, mcap), bf16), v((offs, cb, mcap), bf16), nodes, block, nodes, block,
        v((width, nb), bf16), v((cb, mesh_dev), bf16), v((offs * cb, cap), f32), v((offs, cb, cap), bf16), v((offs, cb, cap), bf16), nodes, block,
        v((width, nb), f32), v((cb, mesh_dev), f32),
        v((cb, grid_dev), bf16), v((width, gb), bf16), v((width, gb), bf16), v((cb, grid_dev), bf16),
        v((fp, cb), bf16), v((fp // 2, cb), bf16), v((fp // 2, cb), bf16), v((inner // 2, fp // inner, cb), bf16),
        v((fp // inner, cb), f32), v((nband // inner, fp // inner, cb), f32), v((fp, cb), bf16),
        pltpu.SemaphoreType.DMA((BATCHES,)), pltpu.SemaphoreType.DMA((BATCHES,)), pltpu.SemaphoreType.DMA((OWN,)),
    ]
    anywhere = pl.BlockSpec(memory_space=pl.ANY)
    results = pl.pallas_call(
        functools.partial(kernel, nband, nchan, inner, scale),
        out_shape=(
            jax.ShapeDtypeStruct((cb, mesh_dev), bf16),
            jax.ShapeDtypeStruct((cb, mesh_dev), f32),
            jax.ShapeDtypeStruct((fp, cb), bf16),
        ),
        in_specs=[anywhere] * len(names),
        out_specs=(anywhere,) * 3,
        scratch_shapes=scratch,
        compiler_params=pltpu.CompilerParams(
            collective_id=0, has_side_effects=True, vmem_limit_bytes=56 * 2**20
        ),
    )(*[a[name] for name in names])
    return pl.pallas_call(
        hand_over,
        out_shape=(
            jax.ShapeDtypeStruct((cb, mesh_dev), bf16),
            jax.ShapeDtypeStruct((cb, mesh_dev), f32),
            jax.ShapeDtypeStruct((fin, cb), f32),
        ),
        in_specs=[anywhere] * 3,
        out_specs=(anywhere,) * 3,
        scratch_shapes=[
            v((cb, mesh_dev), bf16), v((cb, mesh_dev), f32), v((fp, cb), bf16), v((fin, cb), f32),
            pltpu.SemaphoreType.DMA((6,)),
        ],
    )(*results)


def solution(mesh):
    nband, nchan = mesh.shape["band"], mesh.shape["chan"]
    inner = min(16, nband // 2)
    return jax.shard_map(
        functools.partial(local, nband, nchan, inner),
        mesh=mesh,
        in_specs=(
            P(None, "band"),
            P(None, "chan"),
            P("chan", "band"),
            P(None, "band"),
            P("band", None),
            P("band"),
            P("band"),
            P(None, "chan"),
            P(None, "chan"),
            P(None, "chan"),
            P("chan", None),
            P("chan", None),
            P("chan", None),
            P("chan"),
            P(None, "band"),
            P("band", None),
            P("band"),
            P("band"),
            P(None, "chan"),
            P(None, "chan"),
            P(None, "chan"),
            P("chan", None),
            P("chan", None),
            P("chan", None),
            P("chan"),
            P("chan", "band"),
        ),
        out_specs=(P("chan", "band"), P("chan", "band"), P(None, "chan")),
        check_vma=False,
    )
```

```python
import functools

import jax
import jax.numpy as jnp
from jax import lax
from jax.experimental import pallas as pl
from jax.experimental.pallas import tpu as pltpu
from jax.sharding import PartitionSpec as P

eps = 1e-05
bf16 = jnp.bfloat16
f32 = jnp.float32
MESH = pl.DeviceIdType.MESH
BATCHES, OWN = 42, 25
INPUTS = (
    *("grid_in", "w_grid", "mesh_in", "g2m_attr", "g2m_send", "g2m_src", "g2m_dst"),
    *("w_gs", "w_gr", "w_ge", "w_nm", "w_na", "w_no", "gain_enc"),
    *("mesh_attr", "mesh_send", "mesh_src", "mesh_dst"),
    *("w_ms", "w_mr", "w_me", "w_pm", "w_pa", "w_po", "gain_proc", "cotangent"),
)


def whole(f):
    return f[...].reshape(f.shape[0] * f.shape[1], f.shape[2])


def dot(a, b):
    return jnp.dot(a, b, preferred_element_type=f32)


def dot_nt(a, b):
    return lax.dot_general(a, b, (((1,), (1,)), ((), ())), preferred_element_type=f32)


def flip(x):
    return jnp.transpose(x.astype(f32))


def sigmoid(v):
    return 0.5 + 0.5 * jnp.tanh(0.5 * v)


def one_hot(ids, count):
    rows = lax.broadcasted_iota(jnp.int16, (count, ids.shape[1]), 0)
    return jnp.where(rows == ids.astype(jnp.int16), jnp.ones((), bf16), jnp.zeros((), bf16))


def slots_of(ids, capacity, slots):
    slot = jnp.zeros_like(ids)
    for j in range(1, slots):
        slot = slot + (ids >= j * capacity).astype(jnp.int32)
    return slot, ids - slot * capacity


def halves_of(ids, half):
    upper = ids >= half
    return upper, jnp.where(upper, ids - half, ids)


def two_rows(x):
    half = x.shape[1] // 2
    return jnp.concatenate([x[:, :half], x[:, half:]], axis=0)


def norm(out):
    width = out.shape[1]
    mean = jnp.sum(out, axis=1, keepdims=True) / width
    var = jnp.sum(out * out, axis=1, keepdims=True) / width - mean * mean
    inverse = lax.rsqrt(var + eps)
    return (out - mean) * inverse, inverse


def norm_back(grad, normed, inverse, gain):
    width = grad.shape[1]
    u = grad * gain
    a = jnp.sum(u, axis=1, keepdims=True) / width
    b = jnp.sum(u * normed, axis=1, keepdims=True) / width
    return ((u - a - normed * b) * inverse).astype(bf16)


def kernel(
    nband, nchan, inner, scale,
    grid_hbm, w_grid_hbm, mesh_in, g2m_attr_hbm, g2m_send_hbm, g2m_src_hbm, g2m_dst_hbm,
    w_gs_hbm, w_gr_hbm, w_ge_hbm, w_nm, w_na, w_no, gain_enc_hbm,
    mesh_attr_hbm, mesh_send_hbm, mesh_src_hbm, mesh_dst_hbm,
    w_ms, w_mr, w_me_hbm, w_pm, w_pa, w_po, gain_proc_hbm, cotangent,
    mesh_out, mesh_grad, w_grid_sum,
    grid_in, w_grid, g2m_attr, g2m_send, g2m_src, g2m_dst, w_gs, w_gr, w_ge, gain_enc,
    mesh_attr, mesh_send, mesh_src, mesh_dst, w_me, gain_proc,
    gpad, wg_pad, wg_t, we_pad, attr_g, attr_m,
    mesh_full, gains, cot_rows,
    f_all,
    sgrid, s_grid, halo_out, table, edge_grad, edge_back,
    acc, nbuf, enc_g,
    s_out, r_out, s_in, r_in, mid_s, m_halo_out, m_table, m_edge_grad, m_edge_back, m_nbuf, proc_g,
    mo_out, mo_in, dg_out, dg_in, rows_acc, m_back_out, m_back_in, mr_out, mr_in, h_out, h_in,
    de_out, de_in, g_rows_acc, g_back_out, g_back_in, er_out, er_in, mg_out, mg_in,
    dgrid_out, dgrid_in, dpre_out, dpre_in,
    part, pair_in, pair_sum, rs1, mine, rs2, total,
    ssem, rsem, lsem,
):
    d, c = lax.axis_index("band"), lax.axis_index("chan")
    core = lax.rem(d, 2)
    sibling = d + 1 - 2 * core
    width, cb = w_gs.shape
    fin, grid_dev = grid_in.shape
    mesh_dev = mesh_in.shape[1]
    nb = mesh_dev // nchan
    gb = grid_dev // nchan
    half = mesh_dev // 2
    offs, cap = g2m_send.shape
    radius = offs // 2
    ea = w_ge.shape[0]
    f_nm, f_na, f_no, f_ms, f_mr, f_pm, f_pa, f_po, f_gs, f_gr = (
        f_all.at[i] for i in range(10)
    )
    count = [0]
    local_count = [0]
    started = []

    def at(index, size):
        return pl.ds(pl.multiple_of(index * size, size), size)

    def fetch_local(src, dst):
        copy = pltpu.make_async_copy(src, dst, lsem.at[local_count[0]])
        local_count[0] += 1
        copy.start()
        return copy

    def wait_on(whole, i):
        return pltpu.make_async_remote_copy(
            src_ref=whole, dst_ref=whole, send_sem=ssem.at[i], recv_sem=rsem.at[i],
            device_id={"band": sibling}, device_id_type=MESH,
        )

    def send(sends, whole):
        i = count[0]
        count[0] += 1
        for src, dst, target in sends:
            pltpu.make_async_remote_copy(
                src_ref=src, dst_ref=dst, send_sem=ssem.at[i], recv_sem=rsem.at[i],
                device_id=target, device_id_type=MESH,
            ).start()
        batch = (whole, i)
        started.append(batch)
        return batch

    def sent(batch):
        wait_on(*batch).wait_send()
        started[:] = [other for other in started if other is not batch]

    def arrive(batch):
        wait_on(*batch).wait_recv()

    own_w_grid = fetch_local(w_grid_hbm, w_grid)
    own_w_gs = fetch_local(w_gs_hbm, w_gs)
    own_grid = fetch_local(grid_hbm, grid_in)
    own_mesh = fetch_local(mesh_in, mesh_full.at[at(c, cb), :])
    own_rest = [
        fetch_local(src, dst)
        for src, dst in (
            (g2m_send_hbm, g2m_send), (w_gr_hbm, w_gr), (w_ge_hbm, w_ge), (g2m_attr_hbm, g2m_attr),
            (g2m_src_hbm, g2m_src), (g2m_dst_hbm, g2m_dst), (gain_enc_hbm, gain_enc), (gain_proc_hbm, gain_proc),
            (mesh_attr_hbm, mesh_attr), (mesh_send_hbm, mesh_send), (mesh_src_hbm, mesh_src),
            (mesh_dst_hbm, mesh_dst), (w_me_hbm, w_me), (cotangent.at[:, at(c, nb)], cot_rows.at[at(c, cb), :]),
        )
    ]

    def far_first(size):
        return sorted(range(1, size), key=lambda k: -min(k, size - k))

    chan_peers = [lax.rem(c + k, nchan) for k in far_first(nchan)]

    def band_at(offset):
        return lax.rem(d + offset + nband, nband)

    near = [band_at(o) for o in range(-radius, radius + 1) if o != 0]
    group, place = d // inner, lax.rem(d, inner)
    row, rows = place // 2, inner // 2
    row_peers = [lax.rem(row + k, rows) for k in far_first(rows)]
    inner_peers = [group * inner + 2 * p + core for p in row_peers]
    outer = nband // inner
    outer_peers = [lax.rem(group + k, outer) * inner + place for k in far_first(outer)]
    met = near + inner_peers + outer_peers + [sibling]
    barrier = pltpu.get_barrier_semaphore()
    for p in chan_peers:
        pl.semaphore_signal(barrier, inc=1, device_id={"chan": p}, device_id_type=MESH)
    for b in met:
        pl.semaphore_signal(barrier, inc=1, device_id={"band": b}, device_id_type=MESH)

    others = nchan - 1

    def to_chan(src_of, dst, whole):
        return send([(src_of(p), dst, {"chan": p}) for p in chan_peers], whole)

    def swap_rows(src, dst):
        size, lanes = dst.shape[0], src.shape[1]
        batch = to_chan(lambda p: src.at[at(p, size), :], dst.at[:, at(c, lanes)], dst.at[:, : others * lanes])
        dst[:, at(c, lanes)] = src[at(c, size), :]
        return batch

    def swap_lanes(src, dst):
        size, lanes = src.shape[0], dst.shape[1]
        batch = to_chan(lambda p: src.at[:, at(p, lanes)], dst.at[at(c, size), :], dst.at[: others * size, :])
        dst[at(c, size), :] = src[:, at(c, lanes)]
        return batch

    tail = fin // 16 * 16
    wg_pad[tail:, :] = jnp.zeros((wg_pad.shape[0] - tail, cb), bf16)
    own_w_grid.wait()
    wg_pad[0:fin, :] = w_grid[...]
    wg_t[at(c, cb), :] = flip(wg_pad[...]).astype(bf16)
    pl.semaphore_wait(barrier, len(chan_peers) + len(met))

    def wg_half(p):
        return wg_t.at[at(2 * p + core, cb // 2), :]

    wg_copies = [send([(wg_half(c), wg_half(c), {"chan": p})], wg_half(c)) for p in chan_peers]
    gains[c] = jnp.zeros(gains.shape[1:], f32)

    gpad[tail:, :] = jnp.zeros((gpad.shape[0] - tail, grid_dev), bf16)
    own_grid.wait()
    gpad[0:fin, :] = grid_in[...]
    own_w_gs.wait()
    wgs_t = flip(w_gs[...]).astype(bf16)
    own_mesh.wait()
    for copy in own_rest:
        copy.wait()
    for batch in wg_copies:
        sent(batch)
    mesh_copies = to_chan(lambda p: mesh_in, mesh_full.at[at(c, cb), :], mesh_full.at[: others * cb, :])
    gains[c, 0:1, :] = gain_enc[...]
    gains[c, 1:2, :] = gain_proc[...]
    we_pad[...] = jnp.zeros_like(we_pad)
    we_pad[0:ea, :] = w_ge[...].astype(f32)
    wge_t = jnp.transpose(we_pad[...]).astype(bf16)
    we_pad[0:ea, :] = w_me[...].astype(f32)
    wme_t = jnp.transpose(we_pad[...]).astype(bf16)
    attr_g[...] = jnp.zeros_like(attr_g)
    attr_g[0:ea, :] = g2m_attr[...]
    attr_m[...] = jnp.zeros_like(attr_m)
    attr_m[0:ea, :] = mesh_attr[...]
    wgr_t = flip(w_gr[...]).astype(bf16)

    def passed_on():
        for batch, k in zip(wg_copies, far_first(nchan)[::-1]):
            arrive(batch)
            piece = wg_half(lax.rem(c - k + nchan, nchan))
            yield piece, piece, {"band": sibling}


    wg_copies.reverse()
    wg_shared = send(passed_on(), wg_t.at[: others * cb // 2, :])

    def part_of(shard, full, cuts):
        index = group if cuts > 1 else 0
        if shard.shape[0] == cb:
            rows, lanes = at(index, cb // cuts), at(core, width // 2)
            return shard.at[rows, lanes], full.at[c, rows, lanes], full.at[:, rows, lanes], full.at[:, :, lanes]
        blocks = at(core, nchan // 2)
        size = width // 2 // cuts
        if size >= cb:
            blocks, rows = at(core * cuts + index, size // cb), pl.ds(0, cb)
        else:
            first = (core * cuts + index) * size
            blocks, rows = pl.ds(first // cb, 1), pl.ds(pl.multiple_of(lax.rem(first, cb), size), size)
        source = shard.at[at(core * cuts + index, size), :]
        if size >= cb:
            source = [shard.at[at((core * cuts + index) * (size // cb) + n, cb), :] for n in range(size // cb)]
            target = [full.at[(core * cuts + index) * (size // cb) + n, :, at(c, cb)] for n in range(size // cb)]
        else:
            source, target = [source], [full.at[first // cb, rows, at(c, cb)]]
        return source, target, full.at[blocks, rows, :], full.at[at(core, nchan // 2), :, :]

    def listed(x):
        return x if isinstance(x, list) else [x]

    def fetch(pairs, cuts=1):
        sends, regions, halves, own = [], [], [], local_count[0]
        local_count[0] += 1
        for shard, full in pairs:
            src, dst, region, whole = part_of(shard, full, cuts)
            for one, other in zip(listed(src), listed(dst)):
                pltpu.make_async_copy(one, other, lsem.at[own]).start()
                sends += [(one, other, {"chan": p}) for p in chan_peers]
            regions.append(region)
            halves.append(whole)
        unit = cb // 2 // cuts
        size = len(pairs)
        return send(sends, f_all.at[:size, :others, :unit, :]), own, f_all.at[:size, 0, :unit, :], regions, halves

    def fetched(group_copies):
        inbound, own, own_whole, regions, halves = group_copies
        pltpu.make_async_copy(own_whole, own_whole, lsem.at[own]).wait()
        arrive(inbound)
        return regions, halves

    def relay(group_copies):
        regions, halves = fetched(group_copies)
        sends = [(r, r, {"band": b}) for r in regions for b in outer_peers]
        unit = nchan * cb // 2 // outer
        return send(sends, f_all.at[: len(regions), : outer - 1, :unit, :]), halves

    def share(halves):
        return send([(w, w, {"band": sibling}) for w in halves], f_all.at[: len(halves), : nchan // 2, :, :])

    def relayed(relay_copies):
        arrive(relay_copies[0])
        return share(relay_copies[1])

    sent(mesh_copies)
    gain_copies = to_chan(lambda p: gains.at[c], gains.at[c], gains.at[:others])
    group_m = fetch([(w_ms, f_ms), (w_mr, f_mr)], outer)
    group_a = fetch([(w_nm, f_nm), (w_na, f_na), (w_no, f_no)])

    arrive(wg_shared)

    step = min(512, grid_dev)

    @pl.loop(0, grid_dev // step)
    def _(t):
        cols = at(t, step)
        pre = dot(wg_t[...], gpad[:, cols])
        sig = sigmoid(pre)
        sgrid[:, cols] = sig * (1.0 + pre * (1.0 - sig))
        s_grid[:, cols] = dot(wgs_t, (pre * sig).astype(bf16)).astype(bf16)

    order = [j for o in range(radius, 0, -1) for j in (radius - o, radius + o)]
    passes = [order[i : i + 2] for i in range(0, len(order), 2)]

    def pack(field, lists, out, dest):
        def picked(j):
            return dot(field[...], one_hot(lists[j : j + 1, :], field.shape[1])).astype(bf16)

        def block(n):
            return dest.at[n * cb : (n + 1) * cb, :]

        def sends():
            for n, j in enumerate(order):
                out[j] = picked(j)
                yield out.at[j], block(n), {"band": band_at(j - radius)}

        batch = send(sends(), dest.at[: (offs - 1) * cb, :])
        dest[len(order) * cb :, :] = picked(radius)
        return batch

    halo = pack(s_grid, g2m_send, halo_out, table)

    group_b = fetch([(w_pm, f_pm), (w_pa, f_pa), (w_po, f_po)], outer)
    group_c = fetch([(w_gr, f_gr), (w_gs, f_gs)], outer)

    def upper_lower(upper, x):
        return jnp.concatenate([jnp.where(upper, 0.0, x), jnp.where(upper, x, 0.0)], axis=0).astype(bf16)

    def pick_half(upper, pair):
        return jnp.where(upper, pair[cb:], pair[:cb])

    def edges_near(table, recv, w_edge_t, attr, src, dst, grads, tile):
        @pl.loop(0, src.shape[1] // tile)
        def _(t):
            cols = at(t, tile)
            slot, low = slots_of(src[:, cols], table.shape[1], offs)
            upper, node = halves_of(dst[:, cols], half)
            own = dot(table[len(order) * cb :, :], one_hot(low, table.shape[1]))
            pre = jnp.where(slot == radius, own, 0.0) + dot(w_edge_t, attr[:, cols])
            grads[:, cols] = pre + pick_half(upper, dot(recv, one_hot(node, half)))

    def edges_far(table, src, dst, grads, tile):
        acc[...] = jnp.zeros_like(acc)

        @pl.loop(0, src.shape[1] // tile)
        def _(t):
            cols = at(t, tile)
            slot, low = slots_of(src[:, cols], table.shape[1], offs)
            upper, node = halves_of(dst[:, cols], half)
            remote = dot(table[: len(order) * cb, :], one_hot(low, table.shape[1]))
            sender = jnp.zeros((cb, tile), f32)
            for n, j in enumerate(order):
                sender = jnp.where(slot == j, remote[n * cb : (n + 1) * cb, :], sender)
            pre = grads[:, cols] + sender
            sig = sigmoid(pre)
            grads[:, cols] = sig * (1.0 + pre * (1.0 - sig))
            acc[...] += dot_nt(one_hot(node, half), upper_lower(upper, pre * sig))

    def nodes_of(out):
        out[:half, :] = acc[:, :cb].astype(bf16)
        out[half:, :] = acc[:, cb:].astype(bf16)

    def edges_backward(grad, src, dst, grads, back, rows_ref, out, inbound, tile):
        capacity, tiles = rows_ref.shape[0], src.shape[1] // tile
        acc[...] = jnp.zeros_like(acc)
        rows_ref[...] = jnp.zeros_like(rows_ref)
        copies = []

        def add_rows(slots, base, cols, d_pre):
            slot, low = slots_of(src[:, cols], capacity, offs)
            slot = slot.astype(jnp.int16)
            parts = [jnp.where(slot == j, d_pre, jnp.zeros((), bf16)) for j in slots]
            parts = jnp.concatenate(parts, axis=0) if len(parts) > 1 else parts[0]
            rows_ref[:, base : base + len(slots) * cb] += dot_nt(one_hot(low, capacity), parts)

        for i, slots in enumerate(passes):
            base = 2 * i * cb

            @pl.loop(0, tiles)
            def _(t):
                cols = at(t, tile)
                if i == 0:
                    upper, node = halves_of(dst[:, cols], half)
                    d_pre = pick_half(upper, dot(grad, one_hot(node, half))) * grads[:, cols]
                    back[:, cols] = d_pre.astype(bf16)
                add_rows(slots, base, cols, back[:, cols])

            for n, j in enumerate(slots):
                out[j] = rows_ref[:, base + n * cb : base + (n + 1) * cb].astype(bf16)
            sends = [(out.at[j], inbound.at[j], {"band": band_at(radius - j)}) for j in slots]
            copies.append(send(sends, inbound.at[: len(slots)]))

        base = 2 * len(passes) * cb

        @pl.loop(0, tiles)
        def _(t):
            cols = at(t, tile)
            d_pre = back[:, cols]
            upper, node = halves_of(dst[:, cols], half)
            acc[...] += dot_nt(one_hot(node, half), upper_lower(upper, d_pre.astype(f32)))
            add_rows([radius], base, cols, d_pre)

        inbound[radius] = rows_ref[:, base : base + cb].astype(bf16)
        return copies

    tile_g = min(4096, g2m_src.shape[1])
    tile_m = min(4096, mesh_src.shape[1])
    arrive(mesh_copies)
    recv_g = two_rows(dot(wgr_t, mesh_full[...]).astype(bf16))
    edges_near(table, recv_g, wge_t, attr_g, g2m_src, g2m_dst, edge_grad, tile_g)
    m_relay = relay(group_m)
    arrive(halo)
    edges_far(table, g2m_src, g2m_dst, edge_grad, tile_g)
    nodes_of(nbuf)
    enc_copies = swap_rows(nbuf, enc_g)
    a_copies = share(fetched(group_a)[1])
    b_relay = relay(group_b)
    m_copies = relayed(m_relay)

    x = flip(mesh_full[:, at(c, nb)])
    arrive(gain_copies)
    gain_e = jnp.concatenate([gains[k, 0:1, :] for k in range(nchan)], axis=1)
    gain_p = jnp.concatenate([gains[k, 1:2, :] for k in range(nchan)], axis=1)
    arrive(a_copies)

    def mlp(pre, w_o):
        sig = sigmoid(pre)
        out = dot((pre * sig).astype(bf16), whole(w_o))
        normed, inverse = norm(out)
        return sig * (1.0 + pre * (1.0 - sig)), normed, inverse

    pre = dot(x.astype(bf16), whole(f_nm))
    arrive(enc_copies)
    enc_sg, enc_normed, enc_inverse = mlp(pre + dot(enc_g[...], whole(f_na)), f_no)
    mid = (x + enc_normed * gain_e).astype(bf16)
    arrive(m_copies)
    s_out[...] = dot(mid, whole(f_ms)).astype(bf16)
    s_copies = swap_lanes(s_out, s_in)
    r_out[...] = dot(mid, whole(f_mr)).astype(bf16)
    r_copies = swap_lanes(r_out, r_in)

    arrive(s_copies)
    mid_s[...] = flip(s_in[...]).astype(bf16)
    m_halo = pack(mid_s, mesh_send, m_halo_out, m_table)
    arrive(r_copies)
    c_relay = relay(group_c)
    cot_copies = to_chan(
        lambda p: cotangent.at[:, at(p, nb)], cot_rows.at[at(c, cb), :], cot_rows.at[: others * cb, :]
    )
    recv_m = two_rows(flip(r_in[...]).astype(bf16))
    edges_near(m_table, recv_m, wme_t, attr_m, mesh_src, mesh_dst, m_edge_grad, tile_m)
    arrive(m_halo)
    edges_far(m_table, mesh_src, mesh_dst, m_edge_grad, tile_m)
    nodes_of(m_nbuf)
    proc_copies = swap_rows(m_nbuf, proc_g)
    b_copies = relayed(b_relay)
    arrive(cot_copies)
    cot = flip(cot_rows[...])
    arrive(b_copies)
    pre = dot(mid, whole(f_pm))
    arrive(proc_copies)

    proc_sg, proc_normed, proc_inverse = mlp(pre + dot(proc_g[...], whole(f_pa)), f_po)
    d_out = norm_back(cot, proc_normed, proc_inverse, gain_p)
    d_hid = (dot_nt(d_out, whole(f_po)) * proc_sg).astype(bf16)
    dg_out[...] = dot_nt(whole(f_pa), d_hid).astype(bf16)
    dg_copies = swap_rows(dg_out, dg_in)
    c_copies = relayed(c_relay)
    mo_out[...] = flip(mid.astype(f32) + proc_normed * gain_p).astype(bf16)
    d_mid = cot + dot_nt(d_hid, whole(f_pm))
    arrive(dg_copies)
    mo_copies = swap_rows(mo_out, mo_in)
    m_back = edges_backward(
        two_rows(dg_in[...]), mesh_src, mesh_dst, m_edge_grad, m_edge_back,
        rows_acc, m_back_out, m_back_in, tile_m,
    )
    nodes_of(mr_out)
    mr_copies = swap_rows(mr_out, mr_in)

    def gather_back(copies, inbound, add):
        value = add(radius, inbound[radius])
        for slots, batch in zip(passes, copies):
            arrive(batch)
            for j in slots:
                value = value + add(j, inbound[j])
        return value

    h_out[...] = gather_back(
        m_back, m_back_in, lambda j, rows: dot(one_hot(mesh_send[j : j + 1, :], mesh_dev), rows)
    ).astype(bf16)
    h_copies = swap_rows(h_out, h_in)
    arrive(mr_copies)
    d_mid = d_mid + dot_nt(mr_in[...], whole(f_mr))
    arrive(h_copies)
    d_mid = d_mid + dot_nt(h_in[...], whole(f_ms))

    d_out = norm_back(d_mid, enc_normed, enc_inverse, gain_e)
    d_hid = (dot_nt(d_out, whole(f_no)) * enc_sg).astype(bf16)
    de_out[...] = dot_nt(whole(f_na), d_hid).astype(bf16)
    de_copies = swap_rows(de_out, de_in)
    d_mesh = d_mid + dot_nt(d_hid, whole(f_nm))
    arrive(de_copies)

    g_back = edges_backward(
        two_rows(de_in[...]), g2m_src, g2m_dst, edge_grad, edge_back,
        g_rows_acc, g_back_out, g_back_in, tile_g,
    )
    nodes_of(er_out)
    er_copies = swap_rows(er_out, er_in)
    arrive(c_copies)
    dgrid_out[...] = gather_back(
        g_back, g_back_in, lambda j, rows: dot(one_hot(g2m_send[j : j + 1, :], grid_dev), rows)
    ).astype(bf16)
    dgrid_copies = swap_rows(dgrid_out, dgrid_in)
    arrive(er_copies)
    mg_out[...] = jnp.transpose(d_mesh + dot_nt(er_in[...], whole(f_gr)))
    arrive(dgrid_copies)
    dpre_out[...] = (dot_nt(whole(f_gs), dgrid_in[...]) * sgrid[:, at(c, gb)]).astype(bf16)
    dpre_copies = swap_rows(dpre_out, dpre_in)
    arrive(mo_copies)
    outputs = [fetch_local(mo_in, mesh_out)]
    arrive(dpre_copies)

    share_rows, piece = part.shape[0] // 2, part.shape[0] // inner
    part[at(1 - core, share_rows), :] = dot_nt(gpad[at(1 - core, share_rows), :], dpre_in[...]).astype(bf16)
    pair = send([(part.at[at(1 - core, share_rows), :], pair_in, {"band": sibling})], pair_in)
    mg_copies = swap_rows(mg_out, mg_in)
    mine_half = dot_nt(gpad[at(core, share_rows), :], dpre_in[...])
    arrive(pair)
    pair_sum[...] = (mine_half + pair_in[...].astype(f32)).astype(bf16)
    first = send(
        [(pair_sum.at[at(p, piece), :], rs1.at[row], {"band": b}) for p, b in zip(row_peers, inner_peers)],
        rs1.at[: rows - 1],
    )
    rs1[row] = pair_sum[at(row, piece), :]
    arrive(first)
    mine[...] = jnp.sum(rs1[...].astype(f32), axis=0)
    second = send([(mine, rs2.at[group], {"band": b}) for b in outer_peers], rs2.at[: outer - 1])
    rs2[group] = mine[...]
    arrive(mg_copies)
    outputs.append(fetch_local(mg_in, mesh_grad))
    arrive(second)
    own = at(core * rows + row, piece)
    total[own, :] = (jnp.sum(rs2[...], axis=0) * scale).astype(bf16)
    third = send([(total.at[own, :], total.at[own, :], {"band": b}) for b in inner_peers], total.at[: (rows - 1) * piece, :])
    arrive(third)
    done = total.at[at(core, share_rows), :]
    arrive(send([(done, done, {"band": sibling})], done))
    outputs.append(fetch_local(total, w_grid_sum))
    for batch in list(started):
        sent(batch)
    for copy in outputs:
        copy.wait()


def hand_over(
    mesh_out_in, mesh_grad_in, w_grid_sum, mesh_out, mesh_grad, w_grid_grad,
    held_out, held_grad, held_sum, held_w, sems,
):
    def copy(i, src, dst):
        started = pltpu.make_async_copy(src, dst, sems.at[i])
        started.start()
        return started

    grad_in = copy(0, mesh_grad_in, held_grad)
    sum_in = copy(1, w_grid_sum, held_sum)
    out_in = copy(2, mesh_out_in, held_out)
    grad_in.wait()
    grad_out = copy(3, held_grad, mesh_grad)
    sum_in.wait()
    held_w[...] = held_sum[0 : held_w.shape[0], :].astype(f32)
    w_out = copy(4, held_w, w_grid_grad)
    out_in.wait()
    out_out = copy(5, held_out, mesh_out)
    for last in (grad_out, w_out, out_out):
        last.wait()


def local(nband, nchan, inner, *args):
    names = INPUTS
    a = dict(zip(names, args))
    for name in ("g2m_src", "g2m_dst", "mesh_src", "mesh_dst", "gain_enc", "gain_proc"):
        a[name] = a[name].reshape(1, -1)
    fin, grid_dev = a["grid_in"].shape
    width, cb = a["w_gs"].shape
    mesh_dev = a["mesh_in"].shape[1]
    nb, gb = mesh_dev // nchan, grid_dev // nchan
    offs, cap = a["g2m_send"].shape
    mcap = a["mesh_send"].shape[1]
    edges, medges = a["g2m_src"].shape[1], a["mesh_src"].shape[1]
    fp = -(-fin // 128) * 128
    scale = float(grid_dev * nband) ** (-0.5)
    v = pltpu.VMEM
    nodes = v((mesh_dev, cb), bf16)
    block = v((nb, width), bf16)
    held = [
        *("grid_in", "w_grid", "g2m_attr", "g2m_send", "g2m_src", "g2m_dst", "w_gs", "w_gr", "w_ge", "gain_enc"),
        *("mesh_attr", "mesh_send", "mesh_src", "mesh_dst", "w_me", "gain_proc"),
    ]
    scratch = [
        *[v(a[name].shape, a[name].dtype) for name in held],
        v((fp, grid_dev), bf16), v((fp, cb), bf16), v((width, fp), bf16), v((16, cb), f32),
        v((16, edges), bf16), v((16, medges), bf16),
        v((width, mesh_dev), bf16), v((nchan, 8, cb), f32), v((width, nb), bf16),
        v((10, nchan, cb, width), bf16),
        v((width, grid_dev), f32), v((cb, grid_dev), bf16), v((offs, cb, cap), bf16), v((offs * cb, cap), bf16),
        v((cb, edges), f32), v((cb, edges), bf16),
        v((mesh_dev // 2, 2 * cb), f32), nodes, block,
        block, block, nodes, nodes, v((cb, mesh_dev), bf16), v((offs, cb, mcap), bf16), v((offs * cb, mcap), bf16),
        v((cb, medges), f32), v((cb, medges), bf16), nodes, block,
        *[v((width, nb), bf16), v((cb, mesh_dev), bf16)] * 2, v((mcap, offs * cb), f32),
        v((offs, mcap, cb), bf16), v((offs, mcap, cb), bf16), nodes, block, nodes, block,
        v((width, nb), bf16), v((cb, mesh_dev), bf16), v((cap, offs * cb), f32), v((offs, cap, cb), bf16), v((offs, cap, cb), bf16), nodes, block,
        v((width, nb), f32), v((cb, mesh_dev), f32),
        v((grid_dev, cb), bf16), v((gb, width), bf16), v((width, gb), bf16), v((cb, grid_dev), bf16),
        v((fp, cb), bf16), v((fp // 2, cb), bf16), v((fp // 2, cb), bf16), v((inner // 2, fp // inner, cb), bf16),
        v((fp // inner, cb), f32), v((nband // inner, fp // inner, cb), f32), v((fp, cb), bf16),
        pltpu.SemaphoreType.DMA((BATCHES,)), pltpu.SemaphoreType.DMA((BATCHES,)), pltpu.SemaphoreType.DMA((OWN,)),
    ]
    anywhere = pl.BlockSpec(memory_space=pl.ANY)
    results = pl.pallas_call(
        functools.partial(kernel, nband, nchan, inner, scale),
        out_shape=(
            jax.ShapeDtypeStruct((cb, mesh_dev), bf16),
            jax.ShapeDtypeStruct((cb, mesh_dev), f32),
            jax.ShapeDtypeStruct((fp, cb), bf16),
        ),
        in_specs=[anywhere] * len(names),
        out_specs=(anywhere,) * 3,
        scratch_shapes=scratch,
        compiler_params=pltpu.CompilerParams(
            collective_id=0, has_side_effects=True, vmem_limit_bytes=56 * 2**20
        ),
    )(*[a[name] for name in names])
    return pl.pallas_call(
        hand_over,
        out_shape=(
            jax.ShapeDtypeStruct((cb, mesh_dev), bf16),
            jax.ShapeDtypeStruct((cb, mesh_dev), f32),
            jax.ShapeDtypeStruct((fin, cb), f32),
        ),
        in_specs=[anywhere] * 3,
        out_specs=(anywhere,) * 3,
        scratch_shapes=[
            v((cb, mesh_dev), bf16), v((cb, mesh_dev), f32), v((fp, cb), bf16), v((fin, cb), f32),
            pltpu.SemaphoreType.DMA((6,)),
        ],
    )(*results)


def solution(mesh):
    nband, nchan = mesh.shape["band"], mesh.shape["chan"]
    inner = min(16, nband // 2)
    return jax.shard_map(
        functools.partial(local, nband, nchan, inner),
        mesh=mesh,
        in_specs=(
            P(None, "band"),
            P(None, "chan"),
            P("chan", "band"),
            P(None, "band"),
            P("band", None),
            P("band"),
            P("band"),
            P(None, "chan"),
            P(None, "chan"),
            P(None, "chan"),
            P("chan", None),
            P("chan", None),
            P("chan", None),
            P("chan"),
            P(None, "band"),
            P("band", None),
            P("band"),
            P("band"),
            P(None, "chan"),
            P(None, "chan"),
            P(None, "chan"),
            P("chan", None),
            P("chan", None),
            P("chan", None),
            P("chan"),
            P("chan", "band"),
        ),
        out_specs=(P("chan", "band"), P("chan", "band"), P(None, "chan")),
        check_vma=False,
    )
```
